512 devices in a mesh: clip: 16 (over x, y_hi, core), tm: 32 (over y_lo, z).
Axes of the slice: x: 4, y: 8 (y_hi: 2, y_lo: 4; y = y_hi * 4 + y_lo), z: 8, core: 2. Of those that a mesh axis runs over, the one named last changes fastest.
Arguments:
- inputs: bfloat16 [16, 10240, 768], P('clip', 'tm'), may hold values from -6 to 6
- query_states: bfloat16 [16, 10240, 768], P('clip', 'tm'), may hold values from -9 to 9
- key_states: bfloat16 [16, 10240, 768], P('clip', 'tm'), may hold values from -9 to 9
- value_states: bfloat16 [16, 10240, 768], P('clip', 'tm'), may hold values from -6 to 6
- out_grad: bfloat16 [16, 10240, 768], P('clip', 'tm'), may hold values from -1.1953125 to 1.1953125
- first_flags: int32 [16, 32], P('clip'), may hold values from 0 to 1, as said below
- weight: float32 [768, 768], P('tm'), may hold values from -1.2 to 1.2
- moment_one: float32 [768, 768], P('tm'), may hold values from -6 to 6
- moment_two: float32 [768, 768], P('tm'), may hold values from 0.25 to 4
Outputs:
- new_weight: float32 [768, 768], P('tm')
- new_moment_one: float32 [768, 768], P('tm')
- new_moment_two: float32 [768, 768], P('tm')
The draws below stay inside these ranges and needn't reach their ends.
Inputs may be any that keep to these rules, and one draw needn't show every extreme that they name: `first_flags`: the first frame of every sequence has flag 1.
All inputs are finite; a program needn't handle non-finite values.
Results may differ from the reference program's by a relative error of at most 0.0044.
Values may be sent and summed in bfloat16 or wider, within the bound.
A program may use at most 64 MiB of HBM per device.

```python
import math
import jax
import jax.numpy as jnp
from jax import lax

HEAD_DIM = 128
HEADS = 6
DX = 768
FRAME_TOK = 320
ATT = 768
FRAMES = 32
SEQS = 16
TOKENS = 10240


def drawn_pair(key):
    shape = (SEQS, TOKENS, ATT)
    key_part = jnp.clip(jax.random.normal(jax.random.fold_in(key, 11), shape, jnp.float32), -6.0, 6.0)
    query_part = jnp.clip(jax.random.normal(jax.random.fold_in(key, 12), shape, jnp.float32), -6.0, 6.0)
    return (query_part, key_part)


def draw_query_states(key, part):
    return drawn_pair(key)[0].astype(jnp.bfloat16)


def draw_key_states(key, part):
    return drawn_pair(key)[1].astype(jnp.bfloat16)


def draw_first_flags(key, part):
    draws = jax.random.randint(jax.random.fold_in(key, 21), (SEQS, FRAMES), 0, 8)
    flag_rows = jnp.where(draws == 0, 1, 0).astype(jnp.int32)
    return flag_rows.at[:, 0].set(1)


def strengthened(values, rng, source, target, blocks, factor):
    owner, partner = [(jnp.arange(values.shape[dim]) // (values.shape[dim] // blocks)).reshape([-1 if axis == dim else 1 for axis in range(values.ndim)]) for dim in (source, target)]
    chosen = jax.random.permutation(rng, blocks)[partner]
    strong = (owner == chosen) | (owner == (partner + blocks // 2) % blocks)
    return jnp.where(strong, factor * values, values)


def block_scale(rng, extent, split, least, high):
    level, own = 1.0, jax.random.fold_in(rng, 6)
    for dim, shards_of in split:
        steps = jnp.exp(jax.random.uniform(jax.random.fold_in(own, dim), (shards_of,), jnp.float32, least / len(split), high / len(split)))
        level = level * jnp.repeat(steps, extent[dim] // shards_of).reshape([-1 if axis == dim else 1 for axis in range(len(extent))])
    return level


def centred(rng, shape, width, most, cuts=(), kind=jnp.bfloat16):
    drawn = jax.random.normal(rng, shape, jnp.float32) * width
    if len(cuts) > 0:
        drawn = block_scale(rng, shape, cuts, -0.22, 0.18) * drawn
    return jnp.clip(drawn, min=-most, max=most).astype(kind)


def bell_draw_with(rng, shape, width, most, shards, heavy, held_as=jnp.bfloat16):
    array = width * jax.random.normal(rng, shape, jnp.float32)
    if shards:
        array = array * block_scale(rng, shape, shards, -0.22, 0.18)
    return jnp.clip(strengthened(array, jax.random.fold_in(rng, 3), *heavy), -most, most).astype(held_as)


def setup_inputs(seed: int = 0) -> dict:
    key_of = jax.random.split(jax.random.key(seed), 10)
    return {
        "inputs": bell_draw_with(key_of[0], (SEQS, TOKENS, DX), 1.0, 6.0, ((0, 16), (1, 32)), (1, 2, 32, 2.75)),
        "query_states": draw_query_states(jax.random.fold_in(key_of[9], 71), 0),
        "key_states": draw_key_states(jax.random.fold_in(key_of[9], 71), 0),
        "value_states": centred(key_of[3], (SEQS, TOKENS, ATT), 1.0, 6.0, ((0, 16), (1, 32))),
        "out_grad": centred(key_of[4], (SEQS, TOKENS, ATT), 0.2, 1.1953125, ((0, 16), (1, 32))),
        "first_flags": draw_first_flags(jax.random.fold_in(key_of[9], 71), 0),
        "weight": centred(key_of[6], (DX, ATT), 0.2, 1.2, ((0, 32),), jnp.float32),
        "moment_one": centred(key_of[7], (DX, ATT), 1.0, 6.0, ((0, 32),), jnp.float32),
        "moment_two": jnp.clip(jnp.exp(math.log(4.0) - 2.7725887 * jax.random.uniform(key_of[8], (DX, ATT), jnp.float32) ** block_scale(key_of[8], (DX, ATT), ((0, 32),), -0.2, 0.2)), 0.25, 4.0),
    }


beta_one = 0.9
beta_two = 0.95
learn_rate = 0.001
adam_eps = 1e-08
decay_rate = 0.1
step_count = 10.0

def adamw(weight, moment_one, moment_two, gradient):
    new_one = beta_one * moment_one + (1.0 - beta_one) * gradient
    new_two = beta_two * moment_two + (1.0 - beta_two) * gradient * gradient
    corr_one = new_one / (1.0 - beta_one ** step_count)
    corr_two = new_two / (1.0 - beta_two ** step_count)
    new_weight = weight - learn_rate * (corr_one / (jnp.sqrt(corr_two) + adam_eps) + decay_rate * weight)
    return (new_weight, new_one, new_two)

def block_mask(own_flag, prev_flag):
    near_ok = own_flag == 0
    far_ok = jnp.logical_and(near_ok, prev_flag == 0)
    return jnp.concatenate([jnp.broadcast_to(far_ok, (FRAME_TOK,)), jnp.broadcast_to(near_ok, (FRAME_TOK,)), jnp.ones((FRAME_TOK,), bool)])

def window_grad(query_rows, key_window, value_window, grad_rows, allowed):
    scaling = 1.0 / math.sqrt(HEAD_DIM)
    high = lax.Precision.HIGHEST
    query_heads = query_rows.reshape(FRAME_TOK, HEADS, HEAD_DIM).astype(jnp.float32)
    key_heads = key_window.reshape(3 * FRAME_TOK, HEADS, HEAD_DIM).astype(jnp.float32)
    value_heads = value_window.reshape(3 * FRAME_TOK, HEADS, HEAD_DIM).astype(jnp.float32)
    grad_heads = grad_rows.reshape(FRAME_TOK, HEADS, HEAD_DIM).astype(jnp.float32)
    scores = jnp.einsum('qhd,khd->hqk', query_heads, key_heads, precision=high) * scaling
    scores = jnp.where(allowed[None, None, :], scores, -jnp.inf)
    row_max = lax.optimization_barrier(jnp.max(scores, axis=-1, keepdims=True))
    raised = jnp.exp(scores - row_max)
    softmax = raised / lax.optimization_barrier(jnp.sum(raised, axis=-1, keepdims=True))
    dprobs = jnp.einsum('qhd,khd->hqk', grad_heads, value_heads, precision=high)
    row_dot = lax.optimization_barrier(jnp.sum(softmax * dprobs, axis=-1, keepdims=True))
    dscores = (softmax * (dprobs - row_dot) * scaling).astype(jnp.bfloat16)
    window_part = jnp.einsum('hqk,qhd->khd', dscores.astype(jnp.float32), query_heads, precision=high)
    return window_part.reshape(3 * FRAME_TOK, ATT)

def key_gradient(queries, keys_seq, values_seq, grads_seq, flag_seq):
    zero_pad = jnp.zeros((2 * FRAME_TOK, ATT), jnp.bfloat16)
    keys_pad = jnp.concatenate([zero_pad, keys_seq], axis=0)
    values_pad = jnp.concatenate([zero_pad, values_seq], axis=0)
    flag_pad = jnp.concatenate([jnp.ones((1,), jnp.int32), flag_seq.astype(jnp.int32)])

    def one_frame(carry_grad, frame_idx):
        begin = (frame_idx * FRAME_TOK).astype(jnp.int32)
        query_rows = lax.dynamic_slice_in_dim(queries, begin, FRAME_TOK, 0)
        grad_rows = lax.dynamic_slice_in_dim(grads_seq, begin, FRAME_TOK, 0)
        key_window = lax.dynamic_slice_in_dim(keys_pad, begin, 3 * FRAME_TOK, 0)
        value_window = lax.dynamic_slice_in_dim(values_pad, begin, 3 * FRAME_TOK, 0)
        allowed = block_mask(flag_pad[frame_idx + 1], flag_pad[frame_idx])
        window_part = window_grad(query_rows, key_window, value_window, grad_rows, allowed)
        previous = lax.dynamic_slice_in_dim(carry_grad, begin, 3 * FRAME_TOK, 0)
        carry_grad = lax.dynamic_update_slice_in_dim(carry_grad, previous + window_part, begin, 0)
        return (carry_grad, None)
    start_grad = jnp.zeros((TOKENS + 2 * FRAME_TOK, ATT), jnp.float32)
    summed, _ = lax.scan(one_frame, start_grad, jnp.arange(FRAMES, dtype=jnp.int32))
    return summed[2 * FRAME_TOK:].astype(jnp.bfloat16)

def reference(inputs, query_states, key_states, value_states, out_grad, first_flags, weight, moment_one, moment_two):

    def per_seq(accum_grad, seq_idx):
        key_grad = key_gradient(query_states[seq_idx], key_states[seq_idx], value_states[seq_idx], out_grad[seq_idx], first_flags[seq_idx])
        term = lax.dot_general(inputs[seq_idx], key_grad, (((0,), (0,)), ((), ())), preferred_element_type=jnp.float32)
        return (accum_grad + term, None)
    gradient, _ = lax.scan(per_seq, jnp.zeros((DX, ATT), jnp.float32), jnp.arange(SEQS, dtype=jnp.int32))
    return adamw(weight, moment_one, moment_two, gradient)
```

```python
import functools
import math

import jax
import jax.numpy as jnp
from jax import lax
from jax.experimental import pallas as pl
from jax.experimental.pallas import tpu as pltpu
from jax.sharding import PartitionSpec as P

HEAD_DIM = 128
MESH = pl.DeviceIdType.MESH
NEG = -1e30

ZN = 8
YN = 4
CORES = 2

beta_one = 0.9
beta_two = 0.95
learn_rate = 0.001
adam_eps = 1e-08
decay_rate = 0.1
step_count = 10.0


def adamw(weight, moment_one, moment_two, gradient):
    new_one = beta_one * moment_one + (1.0 - beta_one) * gradient
    new_two = beta_two * moment_two + (1.0 - beta_two) * gradient * gradient
    corr_one = new_one / (1.0 - beta_one**step_count)
    corr_two = new_two / (1.0 - beta_two**step_count)
    new_weight = weight - learn_rate * (
        corr_one / (jnp.sqrt(corr_two) + adam_eps) + decay_rate * weight
    )
    return (new_weight, new_one, new_two)


def dot_nt(a, b):
    return lax.dot_general(a, b, (((1,), (1,)), ((), ())), preferred_element_type=jnp.float32)


def dot_nn(a, b):
    return lax.dot_general(a, b, (((1,), (0,)), ((), ())), preferred_element_type=jnp.float32)


def kernel(
    x_hbm, q_hbm, k_hbm, v_hbm, g_hbm, flags,
    grad_out,
    xcat, xt, qo, ko, vo, go, qn, gn, kp, vp,
    e_own, dp_own, own_st, own_st_in, nf_st, nf_st_in, kgn,
    gbuf, a_in, abuf, b_in, bbuf, c_in, cbuf, d_in, ebuf, e_in,
    sem_loc, sem_locx, win_s, win_r, x_s, x_r, os_s, os_r, nf_s, nf_r,
    a_s, a_r, b_s, b_r, c_s, c_r, d_s, d_r, e_s, e_r,
):
    heads, tok, _ = qo.shape
    pairs = heads // CORES
    tm_n = lax.axis_size("tm")
    clip_n = lax.axis_size("clip")
    quads = clip_n // CORES
    t = lax.axis_index("tm")
    c = lax.axis_index("clip")
    core = lax.rem(c, CORES)
    quad = c // CORES
    z = lax.rem(t, ZN)
    y = t // ZN
    has_prev = t > 0
    has_next = t < tm_n - 1
    nxt = jnp.minimum(t + 1, tm_n - 1)
    prv = jnp.maximum(t - 1, 0)
    sibling = c + 1 - 2 * core

    def cols(h):
        return pl.ds(pl.multiple_of(h * HEAD_DIM, HEAD_DIM), HEAD_DIM)

    def remote(src, dst, ssem, rsem, where):
        return pltpu.make_async_remote_copy(
            src_ref=src, dst_ref=dst, send_sem=ssem, recv_sem=rsem,
            device_id=where, device_id_type=MESH,
        )

    def local_copies(h):
        return [
            pltpu.make_async_copy(src.at[0, :, cols(h)], dst.at[h], sem_loc.at[i, h])
            for i, (src, dst) in enumerate(((q_hbm, qo), (k_hbm, ko), (v_hbm, vo), (g_hbm, go)))
        ]

    def ahead(h):
        return [
            remote(src.at[0, :, cols(h)], dst.at[h], win_s.at[i, h], win_r.at[i, h], {"tm": nxt})
            for i, (src, dst) in enumerate(((k_hbm, kp), (v_hbm, vp)))
        ]

    def behind(h):
        return [
            remote(src.at[0, :, cols(h)], dst.at[h], win_s.at[2 + i, h], win_r.at[2 + i, h], {"tm": prv})
            for i, (src, dst) in enumerate(((q_hbm, qn), (g_hbm, gn)))
        ]

    x_copy = remote(x_hbm.at[0], xcat.at[pl.ds(tok, tok)], x_s.at[0], x_r.at[0], {"tm": nxt})
    x_local = pltpu.make_async_copy(x_hbm.at[0], xcat.at[pl.ds(0, tok)], sem_locx.at[0])
    os_copy = remote(own_st, own_st_in, os_s.at[0], os_r.at[0], {"tm": prv})

    def nf_copy(h):
        return remote(nf_st.at[h], nf_st_in.at[h], nf_s.at[h], nf_r.at[h], {"tm": nxt})

    def a_copy(j):
        return remote(gbuf.at[j, 1 - core], a_in.at[j], a_s.at[j], a_r.at[j], {"clip": sibling})

    def b_copy(j, d):
        to = lax.rem(y + d, YN)
        return remote(abuf.at[j, to], b_in.at[j, d - 1], b_s.at[j, d - 1], b_r.at[j, d - 1],
                      {"tm": to * ZN + z})

    def c_copy(j, d):
        to = lax.rem(z + d, ZN)
        return remote(bbuf.at[j, to], c_in.at[j, d - 1], c_s.at[j, d - 1], c_r.at[j, d - 1],
                      {"tm": y * ZN + to})

    def d_copy(j, d):
        to = lax.rem(quad + d, quads)
        return remote(cbuf.at[j], d_in.at[j, d - 1], d_s.at[j, d - 1], d_r.at[j, d - 1],
                      {"clip": to * CORES + core})

    e_copy = remote(ebuf, e_in, e_s.at[0], e_r.at[0], {"clip": sibling})

    def each(lo, hi, fn):
        def step(i, carry):
            fn(i)
            return carry
        lax.fori_loop(lo, hi, step, 0)

    def start_local(h):
        for cp in local_copies(h):
            cp.start()
    each(0, heads, start_local)
    x_local.start()

    bar = pltpu.get_barrier_semaphore()
    def hello(where):
        pl.semaphore_signal(bar, inc=1, device_id=where, device_id_type=MESH)
    @pl.when(has_prev)
    def _():
        hello({"tm": prv})
    @pl.when(has_next)
    def _():
        hello({"tm": nxt})
    hello({"clip": sibling})
    each(1, YN, lambda d: hello({"tm": lax.rem(y + d, YN) * ZN + z}))
    each(1, ZN, lambda d: hello({"tm": y * ZN + lax.rem(z + d, ZN)}))
    each(1, quads, lambda d: hello({"clip": lax.rem(quad + d, quads) * CORES + core}))
    count = 1 + (YN - 1) + (ZN - 1) + (quads - 1)
    pl.semaphore_wait(bar, count + has_prev.astype(jnp.int32) + has_next.astype(jnp.int32))

    def send_window(h):
        @pl.when(has_next)
        def _():
            for cp in ahead(h):
                cp.start()
        @pl.when(has_prev)
        def _():
            for cp in behind(h):
                cp.start()

    @pl.when(has_next)
    def _():
        x_copy.start()
    send_window(0)
    send_window(1)

    @pl.when(jnp.logical_not(has_prev))
    def _():
        kp[...] = jnp.zeros_like(kp)
        vp[...] = jnp.zeros_like(vp)
        xcat[pl.ds(tok, tok), :] = jnp.zeros((tok, xcat.shape[1]), xcat.dtype)
        nf_st_in[...] = jnp.zeros_like(nf_st_in)
        nf_st_in[:, 0:1, :] = jnp.full((heads, 1, nf_st_in.shape[2]), NEG, jnp.float32)

    @pl.when(jnp.logical_not(has_next))
    def _():
        qn[...] = jnp.zeros_like(qn)
        gn[...] = jnp.zeros_like(gn)
        own_st_in[...] = jnp.ones_like(own_st_in)

    scaling = 1.0 / math.sqrt(HEAD_DIM)
    to_log2 = scaling * math.log2(math.e)

    def block(kk, vv, qq, gg):
        s = dot_nt(kk, qq) * to_log2
        m = jnp.max(s, axis=0, keepdims=True)
        e = jnp.exp2(s - m)
        l = jnp.sum(e, axis=0, keepdims=True)
        dp = dot_nt(vv, gg)
        d = jnp.sum(e * dp, axis=0, keepdims=True)
        return e, dp, m, l, d

    def put(ref, h, m, l, d):
        ref[h, 0:1, 0:tok] = m
        ref[h, 1:2, 0:tok] = l
        ref[h, 2:3, 0:tok] = d

    def get(ref, h):
        return ref[h, 0:1, 0:tok], ref[h, 1:2, 0:tok], ref[h, 2:3, 0:tok]

    own_st[...] = jnp.zeros_like(own_st)
    nf_st[...] = jnp.zeros_like(nf_st)

    def own_block(h):
        for cp in local_copies(h):
            cp.wait()
        e, dp, m, l, d = block(ko[h], vo[h], qo[h], go[h])
        e_own[h] = e
        dp_own[h] = dp
        put(own_st, h, m, l, d)
    each(0, heads, own_block)

    @pl.when(has_prev)
    def _():
        os_copy.start()
    @pl.when(has_next)
    def _():
        os_copy.wait_recv()

    fo = flags[0, t]
    fn = flags[0, nxt]
    near_ok = jnp.logical_and(fn == 0, has_next)
    far_ok = jnp.logical_and(jnp.logical_and(near_ok, fo == 0), has_prev)

    def total(ma, la, da, mb, lb, db):
        mt = jnp.maximum(ma, mb)
        fa = jnp.exp2(ma - mt)
        fb = jnp.exp2(mb - mt)
        inv = 1.0 / (fa * la + fb * lb)
        return fa, fb, inv, (fa * da + fb * db) * inv

    def near_far(h):
        @pl.when(h + 2 < heads)
        def _():
            send_window(h + 2)
        @pl.when(has_prev)
        def _():
            for cp in ahead(h):
                cp.wait_recv()
        @pl.when(has_next)
        def _():
            for cp in behind(h):
                cp.wait_recv()
        qq, gg = qn[h], gn[h]
        e1, dp1, m1, l1, d1 = block(ko[h], vo[h], qq, gg)
        e2, dp2, m2, l2, d2 = block(kp[h], vp[h], qq, gg)
        zero = jnp.zeros_like(m1)
        m1p = jnp.where(near_ok, m1, NEG)
        m2p = jnp.where(far_ok, m2, NEG)
        mb = jnp.maximum(m1p, m2p)
        f1 = jnp.where(near_ok, jnp.exp2(m1p - mb), zero)
        f2 = jnp.where(far_ok, jnp.exp2(m2p - mb), zero)
        lb = f1 * l1 + f2 * l2
        db = f1 * d1 + f2 * d2
        put(nf_st, h, mb, lb, db)
        @pl.when(has_next)
        def _():
            nf_copy(h).start()
        ma, la, da = get(own_st_in, h)
        _, fb, inv, delta = total(ma, la, da, mb, lb, db)
        w = fb * inv * scaling
        ds1 = ((e1 * (f1 * w)) * (dp1 - delta)).astype(jnp.bfloat16)
        ds2 = ((e2 * (f2 * w)) * (dp2 - delta)).astype(jnp.bfloat16)
        kgn[h, 0:tok] = dot_nn(ds1, qq)
        kgn[h, tok : 2 * tok] = dot_nn(ds2, qq)

    def finish(h):
        @pl.when(has_prev)
        def _():
            nf_copy(h).wait_recv()
        ma, la, da = get(own_st, h)
        mb, lb, db = get(nf_st_in, h)
        fa, _, inv, delta = total(ma, la, da, mb, lb, db)
        ds = ((e_own[h] * (fa * inv * scaling)) * (dp_own[h] - delta)).astype(jnp.bfloat16)
        kgn[h, 0:tok] = kgn[h, 0:tok] + dot_nn(ds, qo[h])
        grad = dot_nn(xt[...], kgn[h].astype(jnp.bfloat16))
        gbuf[h // CORES, lax.rem(h, CORES)] = grad.astype(jnp.bfloat16).reshape(gbuf.shape[2:])

    f32 = jnp.float32

    def a_finish(j):
        a_copy(j).wait_recv()
        abuf[j] = (gbuf[j, core].astype(f32) + a_in[j].astype(f32)).astype(jnp.bfloat16)
        each(1, YN, lambda d: b_copy(j, d).start())

    def b_finish(j):
        each(1, YN, lambda d: b_copy(j, d).wait_recv())
        acc = abuf[j, y].astype(f32)
        for d in range(YN - 1):
            acc = acc + b_in[j, d].astype(f32)
        bbuf[j] = acc.reshape(bbuf.shape[1:])
        each(1, ZN, lambda d: c_copy(j, d).start())

    def c_finish(j):
        each(1, ZN, lambda d: c_copy(j, d).wait_recv())
        acc = bbuf[j, z]
        for d in range(ZN - 1):
            acc = acc + c_in[j, d]
        cbuf[j] = acc
        each(1, quads, lambda d: d_copy(j, d).start())

    def d_finish(j):
        each(1, quads, lambda d: d_copy(j, d).wait_recv())
        acc = cbuf[j]
        for d in range(quads - 1):
            acc = acc + d_in[j, d]
        ebuf[j] = acc

    def main(h, carry):
        @pl.when(h < heads)
        def _():
            near_far(h)
        @pl.when(h == 0)
        def _():
            x_local.wait()
            @pl.when(has_prev)
            def _():
                x_copy.wait_recv()
            xt[...] = xcat[...].T
        @pl.when(h > 0)
        def _():
            finish(h - 1)
        j = h // 2 - 1
        @pl.when(jnp.logical_and(lax.rem(h, 2) == 0, h > 0))
        def _():
            a_copy(j).start()
        @pl.when(jnp.logical_and(lax.rem(h, 2) == 0, h > 2))
        def _():
            b_finish(j - 1)
        @pl.when(jnp.logical_and(lax.rem(h, 2) == 1, h > 2))
        def _():
            a_finish(j)
        @pl.when(jnp.logical_and(lax.rem(h, 2) == 1, h > 4))
        def _():
            c_finish(j - 1)
        return carry
    lax.fori_loop(0, heads + 1, main, 0)

    last = pairs - 1
    a_finish(last)
    c_finish(last - 1)
    b_finish(last)
    each(0, last, d_finish)
    c_finish(last)
    d_finish(last)
    e_copy.start()
    for j in range(pairs):
        grad_out[:, cols(j * CORES + core)] = ebuf[j]
    e_copy.wait_recv()
    for j in range(pairs):
        grad_out[:, cols(j * CORES + 1 - core)] = e_in[j]

    @pl.when(has_next)
    def _():
        x_copy.wait_send()
        def sent(h):
            for cp in ahead(h):
                cp.wait_send()
            nf_copy(h).wait_send()
        each(0, heads, sent)
    @pl.when(has_prev)
    def _():
        os_copy.wait_send()
        def sent(h):
            for cp in behind(h):
                cp.wait_send()
        each(0, heads, sent)
    def sent_pair(j):
        a_copy(j).wait_send()
        each(1, YN, lambda d: b_copy(j, d).wait_send())
        each(1, ZN, lambda d: c_copy(j, d).wait_send())
        each(1, quads, lambda d: d_copy(j, d).wait_send())
    each(0, pairs, sent_pair)
    e_copy.wait_send()


def body(
    inputs, query_states, key_states, value_states, out_grad, first_flags,
    weight, moment_one, moment_two,
):
    _, tok, width = query_states.shape
    feats = inputs.shape[2]
    heads = width // HEAD_DIM
    pairs = heads // CORES
    rows = weight.shape[0]
    quads = lax.axis_size("clip") // CORES
    per_y = rows * ZN
    bf, f32 = jnp.bfloat16, jnp.float32
    V = pltpu.VMEM
    lanes = (tok + 127) // 128 * 128
    dma = pltpu.SemaphoreType.DMA
    scratch = (
        [V((2 * tok, feats), bf), V((feats, 2 * tok), bf)]
        + [V((heads, tok, HEAD_DIM), bf)] * 8
        + [V((heads, tok, tok), f32)] * 2
        + [V((heads, 8, lanes), f32)] * 4
        + [V((heads, 2 * tok, HEAD_DIM), f32)]
        + [
            V((pairs, CORES, YN, per_y, HEAD_DIM), bf),
            V((pairs, YN, per_y, HEAD_DIM), bf),
            V((pairs, YN, per_y, HEAD_DIM), bf),
            V((pairs, YN - 1, per_y, HEAD_DIM), bf),
            V((pairs, ZN, rows, HEAD_DIM), f32),
            V((pairs, ZN - 1, rows, HEAD_DIM), f32),
            V((pairs, rows, HEAD_DIM), f32),
            V((pairs, quads - 1, rows, HEAD_DIM), f32),
            V((pairs, rows, HEAD_DIM), f32),
            V((pairs, rows, HEAD_DIM), f32),
        ]
        + [dma((4, heads)), dma((1,))]
        + [dma((4, heads))] * 2
        + [dma((1,))] * 2
        + [dma((1,))] * 2
        + [dma((heads,))] * 2
        + [dma((pairs,))] * 2
        + [dma((pairs, YN - 1))] * 2
        + [dma((pairs, ZN - 1))] * 2
        + [dma((pairs, quads - 1))] * 2
        + [dma((1,))] * 2
    )
    gradient = pl.pallas_call(
        kernel,
        out_shape=jax.ShapeDtypeStruct((rows, width), f32),
        in_specs=[pl.BlockSpec(memory_space=pl.ANY)] * 5 + [pl.BlockSpec(memory_space=pltpu.SMEM)],
        out_specs=pl.BlockSpec(memory_space=pltpu.VMEM),
        scratch_shapes=scratch,
        compiler_params=pltpu.CompilerParams(
            collective_id=0, has_side_effects=True, vmem_limit_bytes=48 * 1024 * 1024
        ),
        cost_estimate=pl.CostEstimate(flops=2_000_000_000, bytes_accessed=3_000_000, transcendentals=2_000_000),
    )(inputs, query_states, key_states, value_states, out_grad, first_flags)
    return adamw(weight, moment_one, moment_two, gradient)


def solution(mesh):
    in_specs = (
        P("clip", "tm", None),
        P("clip", "tm", None),
        P("clip", "tm", None),
        P("clip", "tm", None),
        P("clip", "tm", None),
        P("clip", None),
        P("tm", None),
        P("tm", None),
        P("tm", None),
    )
    out_specs = (P("tm", None), P("tm", None), P("tm", None))
    return jax.shard_map(body, mesh=mesh, in_specs=in_specs, out_specs=out_specs, check_vma=False)
```

```python
import functools
import math

import jax
import jax.numpy as jnp
from jax import lax
from jax.experimental import pallas as pl
from jax.experimental.pallas import tpu as pltpu
from jax.sharding import PartitionSpec as P

HEAD_DIM = 128
MESH = pl.DeviceIdType.MESH
NEG = -1e30
VMEM_BYTES = 66_700_000

ZN = 8
YN = 4
YH = 2
CORES = 2
UNITS = ((0, 2), (2, 4), (4, 5), (5, 6))

beta_one = 0.9
beta_two = 0.95
learn_rate = 0.001
adam_eps = 1e-08
decay_rate = 0.1
step_count = 10.0


def adamw(weight, moment_one, moment_two, gradient):
    new_one = beta_one * moment_one + (1.0 - beta_one) * gradient
    new_two = beta_two * moment_two + (1.0 - beta_two) * gradient * gradient
    corr_one = new_one / (1.0 - beta_one**step_count)
    corr_two = new_two / (1.0 - beta_two**step_count)
    new_weight = weight - learn_rate * (
        corr_one / (jnp.sqrt(corr_two) + adam_eps) + decay_rate * weight
    )
    return (new_weight, new_one, new_two)


def dot_nt(a, b):
    return lax.dot_general(a, b, (((1,), (1,)), ((), ())), preferred_element_type=jnp.float32)


def dot_nn(a, b):
    return lax.dot_general(a, b, (((1,), (0,)), ((), ())), preferred_element_type=jnp.float32)


def kernel(
    x_hbm, q_hbm, k_hbm, v_hbm, g_hbm, flags_hbm,
    grad_out,
    flags, xcat, xt, qo, go, qn, gn, kc, vc,
    e_own, dp_own, own_st, own_st_in, nf_st, nf_st_in, kgn, ret, ret_in,
    *rest,
):
    nu = len(UNITS)
    gbuf, a_in, abuf, b_in, bbuf, c_in, cbuf, y_in, d_in = [rest[i * nu : (i + 1) * nu] for i in range(9)]
    (sem_loc, sem_locx, sem_f, win_s, win_r, x_s, x_r, os_s, os_r, nf_s, nf_r,
     ret_s, ret_r, a_s, a_r, b_s, b_r, c_s, c_r, y_s, y_r, d_s, d_r) = rest[9 * nu :]
    heads, tok, _ = qo.shape
    half = ZN // CORES
    rows = grad_out.shape[0]
    part = half * rows
    f32, bf = jnp.float32, jnp.bfloat16
    tm_n = lax.axis_size("tm")
    xn = lax.axis_size("clip") // (CORES * YH)
    ys = YN * YH
    t = lax.axis_index("tm")
    c = lax.axis_index("clip")
    core = lax.rem(c, CORES)
    x = c // (CORES * YH)
    z = lax.rem(t, ZN)
    y = lax.rem(c // CORES, YH) * YN + t // ZN
    y_lo = t // ZN
    holder = z // half == core
    final = jnp.logical_and(holder, x == y_lo)
    has_prev = t > 0
    has_next = t < tm_n - 1
    nxt = jnp.minimum(t + 1, tm_n - 1)
    prv = jnp.maximum(t - 1, 0)
    sibling = c + 1 - 2 * core

    def cols(h):
        return pl.ds(pl.multiple_of(h * HEAD_DIM, HEAD_DIM), HEAD_DIM)

    cut = tok // 2
    own_rows = pl.ds(0, tok)
    prev_rows = pl.ds(tok, tok)

    def remote(src, dst, ssem, rsem, where):
        return pltpu.make_async_remote_copy(
            src_ref=src, dst_ref=dst, send_sem=ssem, recv_sem=rsem,
            device_id=where, device_id_type=MESH,
        )

    def local_copies(h):
        places = (
            (q_hbm, qo.at[h]), (k_hbm, kc.at[h, own_rows]),
            (v_hbm, vc.at[h, own_rows]), (g_hbm, go.at[h]),
        )
        return [
            pltpu.make_async_copy(src.at[0, :, cols(h)], dst, sem_loc.at[i, h])
            for i, (src, dst) in enumerate(places)
        ]

    def ahead(h):
        return [
            remote(src.at[0, :, cols(h)], dst.at[h, prev_rows], win_s.at[i, h], win_r.at[i, h], {"tm": nxt})
            for i, (src, dst) in enumerate(((k_hbm, kc), (v_hbm, vc)))
        ]

    def behind(h):
        return [
            remote(src.at[0, :, cols(h)], dst.at[h], win_s.at[2 + i, h], win_r.at[2 + i, h], {"tm": prv})
            for i, (src, dst) in enumerate(((q_hbm, qn), (g_hbm, gn)))
        ]

    x_copy = remote(x_hbm.at[0, pl.ds(0, cut)], xcat.at[pl.ds(tok, cut)], x_s.at[0], x_r.at[0], {"tm": nxt})
    x_local = pltpu.make_async_copy(x_hbm.at[0], xcat.at[own_rows], sem_locx.at[0])
    f_local = pltpu.make_async_copy(flags_hbm, flags, sem_f.at[0])
    os_copy = remote(own_st, own_st_in, os_s.at[0], os_r.at[0], {"tm": prv})

    def nf_copy(h):
        return remote(nf_st.at[h], nf_st_in.at[h], nf_s.at[h], nf_r.at[h], {"tm": nxt})

    def ret_copy(h):
        return remote(ret.at[h], ret_in.at[h], ret_s.at[h], ret_r.at[h], {"tm": prv})

    def at_y(to):
        return {"clip": (x * YH + to // YN) * CORES + core, "tm": lax.rem(to, YN) * ZN + z}

    def at_z(to):
        return {"tm": y_lo * ZN + to}

    def at_x(d, to_core):
        return {"clip": lax.rem(x + d, xn) * (YH * CORES) + lax.rem(c, YH * CORES) - core + to_core}

    def a_copy(u):
        return remote(gbuf[u].at[1 - core], a_in[u], a_s.at[u], a_r.at[u], {"clip": sibling})

    def b_copy(u, d):
        return remote(abuf[u].at[lax.rem(x + d, xn)], b_in[u].at[d - 1], b_s.at[u, d - 1], b_r.at[u, d - 1], at_x(d, core))

    def c_copy(u, i):
        to = core * half + i
        slot = lax.rem(to - z + ZN - 1, ZN)
        return remote(bbuf[u].at[i], c_in[u].at[slot], c_s.at[u, i], c_r.at[u, slot], at_z(to))

    def c_arrival(u, slot):
        return remote(bbuf[u].at[0], c_in[u].at[slot], c_s.at[u, 0], c_r.at[u, slot], at_z(lax.rem(z + 1, ZN)))

    def y_copy(u, k):
        to = x + k * YN
        slot = lax.rem(to - y + 2 * ys - 1, ys)
        return remote(cbuf[u], y_in[u].at[slot], y_s.at[u, k], y_r.at[u, slot], at_y(to))

    def y_arrival(u, slot):
        return remote(cbuf[u], y_in[u].at[slot], y_s.at[u, 0], y_r.at[u, slot], at_y(lax.rem(y + 1, ys)))

    def d_copy(u, d, to_core):
        return remote(d_in[u], d_in[u], d_s.at[u, d, to_core], d_r.at[u], at_x(d, to_core))

    def d_near(u):
        return remote(d_in[u], d_in[u], d_s.at[u, 0, 0], d_r.at[u], {"clip": sibling})

    def each(lo, hi, fn):
        def step(i, carry):
            fn(i)
            return carry
        lax.fori_loop(lo, hi, step, 0)

    def start_local(h):
        for cp in local_copies(h):
            cp.start()
    each(0, heads, start_local)
    x_local.start()
    f_local.start()

    bar = pltpu.get_barrier_semaphore()
    def hello(where):
        pl.semaphore_signal(bar, inc=1, device_id=where, device_id_type=MESH)
    @pl.when(has_prev)
    def _():
        hello({"tm": prv})
    @pl.when(has_next)
    def _():
        hello({"tm": nxt})
    hello({"clip": sibling})
    each(1, ys, lambda d: hello(at_y(lax.rem(y + d, ys))))
    each(1, ZN, lambda d: hello(at_z(lax.rem(z + d, ZN))))
    for k in range(CORES):
        each(1, xn, lambda d: hello(at_x(d, k)))
    count = 1 + (ys - 1) + (ZN - 1) + CORES * (xn - 1)
    pl.semaphore_wait(bar, count + has_prev.astype(jnp.int32) + has_next.astype(jnp.int32))

    def send_window(h):
        @pl.when(has_next)
        def _():
            for cp in ahead(h):
                cp.start()
        @pl.when(has_prev)
        def _():
            for cp in behind(h):
                cp.start()

    send_window(0)
    @pl.when(has_next)
    def _():
        x_copy.start()
    send_window(1)

    @pl.when(jnp.logical_not(has_prev))
    def _():
        kc[:, tok : 2 * tok, :] = jnp.zeros((heads, tok, HEAD_DIM), bf)
        vc[:, tok : 2 * tok, :] = jnp.zeros((heads, tok, HEAD_DIM), bf)
        xcat[tok : tok + cut, :] = jnp.zeros((cut, xcat.shape[1]), bf)
        nf_st_in[...] = jnp.zeros_like(nf_st_in)
        nf_st_in[:, 0:1, :] = jnp.full((heads, 1, nf_st_in.shape[2]), NEG, f32)

    @pl.when(jnp.logical_not(has_next))
    def _():
        qn[...] = jnp.zeros_like(qn)
        gn[...] = jnp.zeros_like(gn)
        ret_in[...] = jnp.zeros_like(ret_in)
        own_st_in[...] = jnp.ones_like(own_st_in)

    scaling = 1.0 / math.sqrt(HEAD_DIM)
    to_log2 = scaling * math.log2(math.e)

    def stats(s, dp):
        m = jnp.max(s, axis=0, keepdims=True) * to_log2
        e = jnp.exp2(s * to_log2 - m)
        return e, m, jnp.sum(e, axis=0, keepdims=True), jnp.sum(e * dp, axis=0, keepdims=True)

    def put(ref, h, m, l, d):
        ref[h, 0:1, 0:tok] = m
        ref[h, 1:2, 0:tok] = l
        ref[h, 2:3, 0:tok] = d

    def get(ref, h):
        return ref[h, 0:1, 0:tok], ref[h, 1:2, 0:tok], ref[h, 2:3, 0:tok]

    own_st[...] = jnp.zeros_like(own_st)
    nf_st[...] = jnp.zeros_like(nf_st)

    def own_blocks(i):
        pair = (i * 2, i * 2 + 1)
        for h in pair:
            for cp in local_copies(h):
                cp.wait()
        for h in pair:
            s = dot_nt(kc[h, own_rows], qo[h])
            dp = dot_nt(vc[h, own_rows], go[h])
            e, m, l, d = stats(s, dp)
            e_own[h] = e
            dp_own[h] = dp
            put(own_st, h, m, l, d)
    each(0, heads // 2, own_blocks)

    @pl.when(has_prev)
    def _():
        os_copy.start()
    @pl.when(has_next)
    def _():
        os_copy.wait_recv()

    f_local.wait()
    fo = flags[0, t]
    fn = flags[0, nxt]
    near_ok = jnp.logical_and(fn == 0, has_next)
    far_ok = jnp.logical_and(jnp.logical_and(near_ok, fo == 0), has_prev)

    def total(ma, la, da, mb, lb, db):
        mt = jnp.maximum(ma, mb)
        fa = jnp.exp2(ma - mt)
        fb = jnp.exp2(mb - mt)
        inv = 1.0 / (fa * la + fb * lb)
        return fa, fb, inv, (fa * da + fb * db) * inv

    def near_far(h):
        @pl.when(h + 2 < heads)
        def _():
            send_window(h + 2)
        @pl.when(has_prev)
        def _():
            for cp in ahead(h):
                cp.wait_recv()
        @pl.when(has_next)
        def _():
            for cp in behind(h):
                cp.wait_recv()
        qq, gg = qn[h], gn[h]
        s = dot_nt(kc[h], qq)
        dp = dot_nt(vc[h], gg)
        e1, m1, l1, d1 = stats(s[:tok], dp[:tok])
        e2, m2, l2, d2 = stats(s[tok:], dp[tok:])
        zero = jnp.zeros_like(m1)
        m1p = jnp.where(near_ok, m1, NEG)
        m2p = jnp.where(far_ok, m2, NEG)
        mb = jnp.maximum(m1p, m2p)
        f1 = jnp.where(near_ok, jnp.exp2(m1p - mb), zero)
        f2 = jnp.where(far_ok, jnp.exp2(m2p - mb), zero)
        lb = f1 * l1 + f2 * l2
        db = f1 * d1 + f2 * d2
        put(nf_st, h, mb, lb, db)
        @pl.when(has_next)
        def _():
            nf_copy(h).start()
        ma, la, da = get(own_st_in, h)
        _, fb, inv, delta = total(ma, la, da, mb, lb, db)
        w = fb * inv * scaling
        ds1 = ((e1 * (f1 * w)) * (dp[:tok] - delta)).astype(bf)
        ds2 = ((e2 * (f2 * w)) * (dp[tok:] - delta)).astype(bf)
        kg = dot_nn(jnp.concatenate([ds1, ds2], axis=0), qq)
        kgn[h] = kg[: tok + cut]
        ret[h] = kg[tok + cut :].astype(bf)
        @pl.when(has_prev)
        def _():
            ret_copy(h).start()

    def finish(h):
        @pl.when(has_prev)
        def _():
            nf_copy(h).wait_recv()
        @pl.when(has_next)
        def _():
            ret_copy(h).wait_recv()
        ma, la, da = get(own_st, h)
        mb, lb, db = get(nf_st_in, h)
        fa, _, inv, delta = total(ma, la, da, mb, lb, db)
        ds = ((e_own[h] * (fa * inv * scaling)) * (dp_own[h] - delta)).astype(bf)
        own = dot_nn(ds, qo[h])
        back = ret_in[h].astype(f32)
        kg = jnp.concatenate(
            [kgn[h, 0:cut] + own[:cut], kgn[h, cut:tok] + own[cut:] + back, kgn[h, tok : tok + cut]], axis=0
        ).astype(bf)
        grad = dot_nn(xt[...], kg).astype(bf)
        for u, (lo, hi) in enumerate(UNITS):
            @pl.when(jnp.logical_and(h >= lo, h < hi))
            def _():
                for yy in range(YN):
                    for k in range(CORES):
                        at = (yy * CORES + k) * part
                        gbuf[u][k, yy, :, cols(h - lo)] = grad[at : at + part]

    def a_finish(u):
        a_copy(u).wait_recv()
        for yy in range(YN):
            abuf[u][yy] = (gbuf[u][core, yy].astype(f32) + a_in[u][yy].astype(f32)).astype(bf)
        each(1, xn, lambda d: b_copy(u, d).start())

    def b_finish(u):
        each(1, xn, lambda d: b_copy(u, d).wait_recv())
        acc = abuf[u][x].astype(f32)
        for d in range(xn - 1):
            acc = acc + b_in[u][d].astype(f32)
        bbuf[u][...] = acc.reshape(bbuf[u].shape)
        def send(i):
            @pl.when(core * half + i != z)
            def _():
                c_copy(u, i).start()
        each(0, half, send)

    def c_finish(u):
        @pl.when(holder)
        def _():
            each(0, ZN - 1, lambda i: c_arrival(u, i).wait_recv())
            acc = bbuf[u][lax.rem(z, half)]
            for i in range(ZN - 1):
                acc = acc + c_in[u][i]
            cbuf[u][...] = acc
            def send(k):
                @pl.when(x + k * YN != y)
                def _():
                    y_copy(u, k).start()
            each(0, YH, send)

    def y_finish(u):
        @pl.when(final)
        def _():
            each(0, ys - 1, lambda i: y_arrival(u, i).wait_recv())
            acc = cbuf[u][...]
            for i in range(ys - 1):
                acc = acc + y_in[u][i]
            d_in[u][...] = acc
            d_near(u).start()
            for k in range(CORES):
                each(1, xn, lambda d: d_copy(u, d, k).start())

    def d_finish(u):
        @pl.when(jnp.logical_not(final))
        def _():
            d_near(u).wait_recv()
        lo, hi = UNITS[u]
        grad_out[:, lo * HEAD_DIM : hi * HEAD_DIM] = d_in[u][...]

    def main(h, carry):
        @pl.when(h < heads)
        def _():
            near_far(h)
        @pl.when(h == 0)
        def _():
            x_local.wait()
            @pl.when(has_prev)
            def _():
                x_copy.wait_recv()
            xt[...] = xcat[...].T
        @pl.when(h == 6)
        def _():
            a_finish(2)
        @pl.when(h > 0)
        def _():
            finish(h - 1)
        @pl.when(h == 2)
        def _():
            a_copy(0).start()
        @pl.when(h == 3)
        def _():
            a_finish(0)
        @pl.when(h == 4)
        def _():
            a_copy(1).start()
        @pl.when(h == 5)
        def _():
            a_copy(2).start()
            a_finish(1)
            b_finish(0)
        return carry
    lax.fori_loop(0, heads + 1, main, 0)

    a_copy(3).start()
    b_finish(1)
    c_finish(0)
    a_finish(3)
    b_finish(2)
    y_finish(0)
    c_finish(1)
    b_finish(3)
    c_finish(2)
    y_finish(1)
    c_finish(3)
    y_finish(2)
    d_finish(0)
    d_finish(1)
    y_finish(3)
    d_finish(2)
    d_finish(3)

    @pl.when(has_next)
    def _():
        x_copy.wait_send()
        def sent(h):
            for cp in ahead(h):
                cp.wait_send()
            nf_copy(h).wait_send()
        each(0, heads, sent)
    @pl.when(has_prev)
    def _():
        os_copy.wait_send()
        def sent(h):
            for cp in behind(h):
                cp.wait_send()
            ret_copy(h).wait_send()
        each(0, heads, sent)
    for u in range(nu):
        a_copy(u).wait_send()
        each(1, xn, lambda d: b_copy(u, d).wait_send())
        def left(i):
            @pl.when(core * half + i != z)
            def _():
                c_copy(u, i).wait_send()
        each(0, half, left)
        @pl.when(holder)
        def _():
            def left_y(k):
                @pl.when(x + k * YN != y)
                def _():
                    y_copy(u, k).wait_send()
            each(0, YH, left_y)
        @pl.when(final)
        def _():
            d_near(u).wait_send()
            for k in range(CORES):
                each(1, xn, lambda d: d_copy(u, d, k).wait_send())


def body(
    inputs, query_states, key_states, value_states, out_grad, first_flags,
    weight, moment_one, moment_two,
):
    _, tok, width = query_states.shape
    feats = inputs.shape[2]
    heads = width // HEAD_DIM
    rows = weight.shape[0]
    xn = lax.axis_size("clip") // (CORES * YH)
    ys = YN * YH
    half = ZN // CORES
    part = half * rows
    wide = [(hi - lo) * HEAD_DIM for lo, hi in UNITS]
    nu = len(UNITS)
    bf, f32 = jnp.bfloat16, jnp.float32
    V = pltpu.VMEM
    lanes = (tok + 127) // 128 * 128
    dma = pltpu.SemaphoreType.DMA
    scratch = (
        [pltpu.SMEM(first_flags.shape, jnp.int32)]
        + [V((tok + tok // 2, feats), bf), V((feats, tok + tok // 2), bf)]
        + [V((heads, tok, HEAD_DIM), bf)] * 4
        + [V((heads, 2 * tok, HEAD_DIM), bf)] * 2
        + [V((heads, tok, tok), f32)] * 2
        + [V((heads, 8, lanes), f32)] * 4
        + [V((heads, tok + tok // 2, HEAD_DIM), f32)]
        + [V((heads, tok // 2, HEAD_DIM), bf)] * 2
        + [V((CORES, YN, part, w), bf) for w in wide]
        + [V((YN, part, w), bf) for w in wide]
        + [V((YN, part, w), bf) for w in wide]
        + [V((xn - 1, part, w), bf) for w in wide]
        + [V((half, rows, w), f32) for w in wide]
        + [V((ZN - 1, rows, w), f32) for w in wide]
        + [V((rows, w), f32) for w in wide]
        + [V((ys - 1, rows, w), f32) for w in wide]
        + [V((rows, w), f32) for w in wide]
        + [dma((4, heads)), dma((1,)), dma((1,))]
        + [dma((4, heads))] * 2
        + [dma((1,))] * 2
        + [dma((1,))] * 2
        + [dma((heads,))] * 4
        + [dma((nu,))] * 2
        + [dma((nu, xn - 1))] * 2
        + [dma((nu, half)), dma((nu, ZN - 1))]
        + [dma((nu, YH)), dma((nu, ys - 1))]
        + [dma((nu, xn, CORES)), dma((nu,))]
    )
    gradient = pl.pallas_call(
        kernel,
        out_shape=jax.ShapeDtypeStruct((rows, width), f32),
        in_specs=[pl.BlockSpec(memory_space=pltpu.HBM)] * 6,
        out_specs=pl.BlockSpec(memory_space=pltpu.VMEM),
        scratch_shapes=scratch,
        compiler_params=pltpu.CompilerParams(
            collective_id=0, has_side_effects=True, vmem_limit_bytes=VMEM_BYTES
        ),
        cost_estimate=pl.CostEstimate(flops=2_000_000_000, bytes_accessed=3_000_000, transcendentals=2_000_000),
    )(inputs, query_states, key_states, value_states, out_grad, first_flags)
    return adamw(weight, moment_one, moment_two, gradient)


def solution(mesh):
    in_specs = (
        P("clip", "tm", None),
        P("clip", "tm", None),
        P("clip", "tm", None),
        P("clip", "tm", None),
        P("clip", "tm", None),
        P("clip", None),
        P("tm", None),
        P("tm", None),
        P("tm", None),
    )
    out_specs = (P("tm", None), P("tm", None), P("tm", None))
    return jax.shard_map(body, mesh=mesh, in_specs=in_specs, out_specs=out_specs, check_vma=False)
```

```python
import functools
import math

import jax
import jax.numpy as jnp
from jax import lax
from jax.experimental import pallas as pl
from jax.experimental.pallas import tpu as pltpu
from jax.sharding import PartitionSpec as P

HEAD_DIM = 128
MESH = pl.DeviceIdType.MESH
NEG = -1e30
VMEM_BYTES = 66_700_000

ZN = 8
YN = 4
YH = 2
CORES = 2
ROUNDS = 3
UNITS = ((0, 2), (2, 4), (4, 5), (5, 6))

beta_one = 0.9
beta_two = 0.95
learn_rate = 0.001
adam_eps = 1e-08
decay_rate = 0.1
step_count = 10.0


def adamw(weight, moment_one, moment_two, gradient):
    new_one = beta_one * moment_one + (1.0 - beta_one) * gradient
    new_two = beta_two * moment_two + (1.0 - beta_two) * gradient * gradient
    corr_one = new_one / (1.0 - beta_one**step_count)
    corr_two = new_two / (1.0 - beta_two**step_count)
    new_weight = weight - learn_rate * (
        corr_one / (jnp.sqrt(corr_two) + adam_eps) + decay_rate * weight
    )
    return (new_weight, new_one, new_two)


def dot_nt(a, b):
    return lax.dot_general(a, b, (((1,), (1,)), ((), ())), preferred_element_type=jnp.float32)


def dot_nn(a, b):
    return lax.dot_general(a, b, (((1,), (0,)), ((), ())), preferred_element_type=jnp.float32)


def kernel(
    x_hbm, q_hbm, k_hbm, v_hbm, g_hbm, flags_hbm,
    grad_out,
    flags, xcat, xt, qo, go, qn, gn, kc, vc,
    e_own, dp_own, own_st, own_st_in, nf_st, nf_st_in, kgn, ret, ret_in,
    *rest,
):
    nu = len(UNITS)
    gbuf, a_in, abuf, b_in, bbuf, c_in, cbuf, y_in, d_in = [rest[i * nu : (i + 1) * nu] for i in range(9)]
    (sem_loc, sem_locx, sem_f, win_s, win_r, x_s, x_r, os_s, os_r, nf_s, nf_r,
     near_sem, ret_s, ret_r, a_s, a_r, b_s, b_r, c_s, c_r, y_s, y_r, d_s, d_r) = rest[9 * nu :]
    heads, tok, _ = qo.shape
    half = ZN // CORES
    rows = grad_out.shape[0]
    part = half * rows
    f32, bf = jnp.float32, jnp.bfloat16
    tm_n = lax.axis_size("tm")
    xn = lax.axis_size("clip") // (CORES * YH)
    ys = YN * YH
    t = lax.axis_index("tm")
    c = lax.axis_index("clip")
    core = lax.rem(c, CORES)
    x = c // (CORES * YH)
    z = lax.rem(t, ZN)
    y = lax.rem(c // CORES, YH) * YN + t // ZN
    y_lo = t // ZN
    holder = z // half == core
    final = jnp.logical_and(holder, x == y_lo)
    has_prev = t > 0
    has_next = t < tm_n - 1
    nxt = jnp.minimum(t + 1, tm_n - 1)
    prv = jnp.maximum(t - 1, 0)
    sibling = c + 1 - 2 * core

    def cols(h):
        return pl.ds(pl.multiple_of(h * HEAD_DIM, HEAD_DIM), HEAD_DIM)

    cut = tok // 2
    own_rows = pl.ds(0, tok)
    prev_rows = pl.ds(tok, tok)

    def remote(src, dst, ssem, rsem, where):
        return pltpu.make_async_remote_copy(
            src_ref=src, dst_ref=dst, send_sem=ssem, recv_sem=rsem,
            device_id=where, device_id_type=MESH,
        )

    def local_copies(h):
        places = (
            (q_hbm, qo.at[h]), (k_hbm, kc.at[h, own_rows]),
            (v_hbm, vc.at[h, own_rows]), (g_hbm, go.at[h]),
        )
        return [
            pltpu.make_async_copy(src.at[0, :, cols(h)], dst, sem_loc.at[i, h])
            for i, (src, dst) in enumerate(places)
        ]

    def ahead(h):
        return [
            remote(src.at[0, :, cols(h)], dst.at[h, prev_rows], win_s.at[i, h], win_r.at[i, h], {"tm": nxt})
            for i, (src, dst) in enumerate(((k_hbm, kc), (v_hbm, vc)))
        ]

    def behind(h):
        return [
            remote(src.at[0, :, cols(h)], dst.at[h], win_s.at[2 + i, h], win_r.at[2 + i, h], {"tm": prv})
            for i, (src, dst) in enumerate(((q_hbm, qn), (g_hbm, gn)))
        ]

    x_copy = remote(x_hbm.at[0, pl.ds(0, cut)], xcat.at[pl.ds(tok, cut)], x_s.at[0], x_r.at[0], {"tm": nxt})
    x_local = pltpu.make_async_copy(x_hbm.at[0], xcat.at[own_rows], sem_locx.at[0])
    f_local = pltpu.make_async_copy(flags_hbm, flags, sem_f.at[0])
    os_copy = remote(own_st, own_st_in, os_s.at[0], os_r.at[0], {"tm": prv})

    def nf_copy(h):
        return remote(nf_st.at[h], nf_st_in.at[h], nf_s.at[h], nf_r.at[h], {"tm": nxt})

    def ret_copy(h):
        return remote(ret.at[h], ret_in.at[h], ret_s.at[h], ret_r.at[h], {"tm": prv})

    def at_y(to):
        return {"clip": (x * YH + to // YN) * CORES + core, "tm": lax.rem(to, YN) * ZN + z}

    def at_z(to):
        return {"tm": y_lo * ZN + to}

    def at_x(d, to_core):
        return {"clip": lax.rem(x + d, xn) * (YH * CORES) + lax.rem(c, YH * CORES) - core + to_core}

    def a_copy(u):
        return remote(gbuf[u].at[1 - core], a_in[u], a_s.at[u], a_r.at[u], {"clip": sibling})

    def b_copy(u, d):
        return remote(abuf[u].at[lax.rem(x + d, xn)], b_in[u].at[d - 1], b_s.at[u, d - 1], b_r.at[u, d - 1], at_x(d, core))

    def c_copy(u, i):
        to = core * half + i
        slot = lax.rem(to - z + ZN - 1, ZN)
        return remote(bbuf[u].at[i], c_in[u].at[slot], c_s.at[u, i], c_r.at[u, slot], at_z(to))

    def c_arrival(u, slot):
        return remote(bbuf[u].at[0], c_in[u].at[slot], c_s.at[u, 0], c_r.at[u, slot], at_z(lax.rem(z + 1, ZN)))

    def y_copy(u, k):
        to = x + k * YN
        slot = lax.rem(to - y + 2 * ys - 1, ys)
        return remote(cbuf[u], y_in[u].at[slot], y_s.at[u, k], y_r.at[u, slot], at_y(to))

    def y_arrival(u, slot):
        return remote(cbuf[u], y_in[u].at[slot], y_s.at[u, 0], y_r.at[u, slot], at_y(lax.rem(y + 1, ys)))

    def d_copy(u, d, to_core):
        return remote(d_in[u], d_in[u], d_s.at[u, d, to_core], d_r.at[u], at_x(d, to_core))

    def d_near(u):
        return remote(d_in[u], d_in[u], d_s.at[u, 0, 0], d_r.at[u], {"clip": sibling})

    def each(lo, hi, fn):
        def step(i, carry):
            fn(i)
            return carry
        lax.fori_loop(lo, hi, step, 0)

    def start_local(h):
        for cp in local_copies(h):
            cp.start()
    bar = pltpu.get_barrier_semaphore()
    def hello(where):
        pl.semaphore_signal(bar, inc=1, device_id=where, device_id_type=MESH)
    @pl.when(has_prev)
    def _():
        hello({"tm": prv})
    @pl.when(has_next)
    def _():
        hello({"tm": nxt})
    hello({"clip": sibling})
    beside = [
        at_z(lax.rem(z + 1, ZN)), at_z(lax.rem(z + ZN - 1, ZN)),
        at_y(lax.rem(y + 1, ys)), at_y(lax.rem(y + ys - 1, ys)),
        at_x(1, core), at_x(xn - 1, core),
    ]
    for where in beside:
        hello(where)
    count = 1 + len(beside)
    each(0, heads, start_local)
    x_local.start()
    f_local.start()
    pl.semaphore_wait(bar, count + has_prev.astype(jnp.int32) + has_next.astype(jnp.int32))

    def tell(i):
        for where in beside:
            pl.semaphore_signal(near_sem.at[i], inc=1, device_id=where, device_id_type=MESH)

    def hear(i):
        pl.semaphore_wait(near_sem.at[i], len(beside))

    def send_window(h):
        @pl.when(has_next)
        def _():
            for cp in ahead(h):
                cp.start()
        @pl.when(has_prev)
        def _():
            for cp in behind(h):
                cp.start()

    send_window(0)
    @pl.when(has_next)
    def _():
        x_copy.start()
    send_window(1)
    tell(0)

    @pl.when(jnp.logical_not(has_prev))
    def _():
        kc[:, tok : 2 * tok, :] = jnp.zeros((heads, tok, HEAD_DIM), bf)
        vc[:, tok : 2 * tok, :] = jnp.zeros((heads, tok, HEAD_DIM), bf)
        xcat[tok : tok + cut, :] = jnp.zeros((cut, xcat.shape[1]), bf)
        nf_st_in[...] = jnp.zeros_like(nf_st_in)
        nf_st_in[:, 0:1, :] = jnp.full((heads, 1, nf_st_in.shape[2]), NEG, f32)

    @pl.when(jnp.logical_not(has_next))
    def _():
        qn[...] = jnp.zeros_like(qn)
        gn[...] = jnp.zeros_like(gn)
        ret_in[...] = jnp.zeros_like(ret_in)
        own_st_in[...] = jnp.ones_like(own_st_in)

    scaling = 1.0 / math.sqrt(HEAD_DIM)
    to_log2 = scaling * math.log2(math.e)

    def stats(s, dp):
        m = jnp.max(s, axis=0, keepdims=True) * to_log2
        e = jnp.exp2(s * to_log2 - m)
        return e, m, jnp.sum(e, axis=0, keepdims=True), jnp.sum(e * dp, axis=0, keepdims=True)

    def put(ref, h, m, l, d):
        ref[h, 0:1, 0:tok] = m
        ref[h, 1:2, 0:tok] = l
        ref[h, 2:3, 0:tok] = d

    def get(ref, h):
        return ref[h, 0:1, 0:tok], ref[h, 1:2, 0:tok], ref[h, 2:3, 0:tok]

    own_st[...] = jnp.zeros_like(own_st)
    nf_st[...] = jnp.zeros_like(nf_st)

    def own_blocks(i):
        pair = (i * 2, i * 2 + 1)
        for h in pair:
            for cp in local_copies(h):
                cp.wait()
        for h in pair:
            s = dot_nt(kc[h, own_rows], qo[h])
            dp = dot_nt(vc[h, own_rows], go[h])
            e, m, l, d = stats(s, dp)
            e_own[h] = e
            dp_own[h] = dp
            put(own_st, h, m, l, d)
    each(0, heads // 2, own_blocks)

    @pl.when(has_prev)
    def _():
        os_copy.start()
    send_window(2)

    f_local.wait()
    fo = flags[0, t]
    fn = flags[0, nxt]
    near_ok = jnp.logical_and(fn == 0, has_next)
    far_ok = jnp.logical_and(jnp.logical_and(near_ok, fo == 0), has_prev)

    def total(ma, la, da, mb, lb, db):
        mt = jnp.maximum(ma, mb)
        fa = jnp.exp2(ma - mt)
        fb = jnp.exp2(mb - mt)
        inv = 1.0 / (fa * la + fb * lb)
        return fa, fb, inv, (fa * da + fb * db) * inv

    def near_far(h):
        @pl.when(has_prev)
        def _():
            for cp in ahead(h):
                cp.wait_recv()
        @pl.when(has_next)
        def _():
            for cp in behind(h):
                cp.wait_recv()
        qq, gg = qn[h], gn[h]
        s = dot_nt(kc[h], qq)
        dp = dot_nt(vc[h], gg)
        e1, m1, l1, d1 = stats(s[:tok], dp[:tok])
        e2, m2, l2, d2 = stats(s[tok:], dp[tok:])
        zero = jnp.zeros_like(m1)
        m1p = jnp.where(near_ok, m1, NEG)
        m2p = jnp.where(far_ok, m2, NEG)
        mb = jnp.maximum(m1p, m2p)
        f1 = jnp.where(near_ok, jnp.exp2(m1p - mb), zero)
        f2 = jnp.where(far_ok, jnp.exp2(m2p - mb), zero)
        lb = f1 * l1 + f2 * l2
        db = f1 * d1 + f2 * d2
        put(nf_st, h, mb, lb, db)
        @pl.when(has_next)
        def _():
            nf_copy(h).start()
        @pl.when(jnp.logical_and(h == 0, has_next))
        def _():
            os_copy.wait_recv()
        ma, la, da = get(own_st_in, h)
        _, fb, inv, delta = total(ma, la, da, mb, lb, db)
        w = fb * inv * scaling
        ds1 = ((e1 * (f1 * w)) * (dp[:tok] - delta)).astype(bf)
        ds2 = ((e2 * (f2 * w)) * (dp[tok:] - delta)).astype(bf)
        kg = dot_nn(jnp.concatenate([ds1, ds2], axis=0), qq)
        kgn[h] = kg[: tok + cut]
        ret[h] = kg[tok + cut :].astype(bf)
        @pl.when(has_prev)
        def _():
            ret_copy(h).start()
        @pl.when(h + 3 < heads)
        def _():
            send_window(h + 3)

    def finish(h):
        @pl.when(has_prev)
        def _():
            nf_copy(h).wait_recv()
        ma, la, da = get(own_st, h)
        mb, lb, db = get(nf_st_in, h)
        fa, _, inv, delta = total(ma, la, da, mb, lb, db)
        ds = ((e_own[h] * (fa * inv * scaling)) * (dp_own[h] - delta)).astype(bf)
        own = dot_nn(ds, qo[h])
        @pl.when(has_next)
        def _():
            ret_copy(h).wait_recv()
        back = ret_in[h].astype(f32)
        kg = jnp.concatenate(
            [kgn[h, 0:cut] + own[:cut], kgn[h, cut:tok] + own[cut:] + back, kgn[h, tok : tok + cut]], axis=0
        ).astype(bf)
        grad = dot_nn(xt[...], kg).astype(bf)
        for u, (lo, hi) in enumerate(UNITS):
            @pl.when(jnp.logical_and(h >= lo, h < hi))
            def _():
                for yy in range(YN):
                    for k in range(CORES):
                        at = (yy * CORES + k) * part
                        gbuf[u][k, yy, :, cols(h - lo)] = grad[at : at + part]

    def a_finish(u):
        a_copy(u).wait_recv()
        for yy in range(YN):
            abuf[u][yy] = (gbuf[u][core, yy].astype(f32) + a_in[u][yy].astype(f32)).astype(bf)
        each(1, xn, lambda d: b_copy(u, d).start())

    def b_finish(u):
        each(1, xn, lambda d: b_copy(u, d).wait_recv())
        acc = abuf[u][x].astype(f32)
        for d in range(xn - 1):
            acc = acc + b_in[u][d].astype(f32)
        bbuf[u][...] = acc.reshape(bbuf[u].shape)
        def send(i):
            @pl.when(core * half + i != z)
            def _():
                c_copy(u, i).start()
        each(0, half, send)

    def c_finish(u):
        @pl.when(holder)
        def _():
            each(0, ZN - 1, lambda i: c_arrival(u, i).wait_recv())
            acc = bbuf[u][lax.rem(z, half)]
            for i in range(ZN - 1):
                acc = acc + c_in[u][i]
            cbuf[u][...] = acc
            def send(k):
                @pl.when(x + k * YN != y)
                def _():
                    y_copy(u, k).start()
            each(0, YH, send)

    def y_finish(u):
        @pl.when(final)
        def _():
            each(0, ys - 1, lambda i: y_arrival(u, i).wait_recv())
            acc = cbuf[u][...]
            for i in range(ys - 1):
                acc = acc + y_in[u][i]
            d_in[u][...] = acc
            d_near(u).start()
            for k in range(CORES):
                each(1, xn, lambda d: d_copy(u, d, k).start())

    def d_finish(u):
        @pl.when(jnp.logical_not(final))
        def _():
            d_near(u).wait_recv()
        lo, hi = UNITS[u]
        grad_out[:, lo * HEAD_DIM : hi * HEAD_DIM] = d_in[u][...]

    def main(h, carry):
        @pl.when(h < heads)
        def _():
            near_far(h)
        @pl.when(h == 0)
        def _():
            x_local.wait()
            @pl.when(has_prev)
            def _():
                x_copy.wait_recv()
            xt[...] = xcat[...].T
        @pl.when(h == 6)
        def _():
            a_finish(2)
        @pl.when(h > 0)
        def _():
            finish(h - 1)
        @pl.when(h < ROUNDS)
        def _():
            hear(h)
        @pl.when(h < ROUNDS - 1)
        def _():
            tell(h + 1)
        @pl.when(h == 2)
        def _():
            a_copy(0).start()
        @pl.when(h == 3)
        def _():
            a_finish(0)
        @pl.when(h == 4)
        def _():
            a_copy(1).start()
        @pl.when(h == 5)
        def _():
            a_copy(2).start()
            a_finish(1)
        return carry
    lax.fori_loop(0, heads + 1, main, 0)

    def sent_window():
        @pl.when(has_next)
        def _():
            x_copy.wait_send()
            def sent(h):
                for cp in ahead(h):
                    cp.wait_send()
                nf_copy(h).wait_send()
            each(0, heads, sent)
        @pl.when(has_prev)
        def _():
            os_copy.wait_send()
            def sent(h):
                for cp in behind(h):
                    cp.wait_send()
                ret_copy(h).wait_send()
            each(0, heads, sent)

    def sent_ab(u):
        a_copy(u).wait_send()
        each(1, xn, lambda d: b_copy(u, d).wait_send())

    def sent_c(u):
        def left(i):
            @pl.when(core * half + i != z)
            def _():
                c_copy(u, i).wait_send()
        each(0, half, left)

    def sent_y(u):
        @pl.when(holder)
        def _():
            def left(k):
                @pl.when(x + k * YN != y)
                def _():
                    y_copy(u, k).wait_send()
            each(0, YH, left)

    def sent_d(u):
        @pl.when(final)
        def _():
            d_near(u).wait_send()
            for k in range(CORES):
                each(1, xn, lambda d: d_copy(u, d, k).wait_send())

    last = nu - 1
    a_copy(last).start()
    sent_window()
    b_finish(0)
    b_finish(1)
    a_finish(last)
    b_finish(2)
    for u in range(last):
        sent_ab(u)
    c_finish(0)
    c_finish(1)
    b_finish(last)
    c_finish(2)
    sent_ab(last)
    for u in range(last):
        sent_c(u)
    y_finish(0)
    y_finish(1)
    c_finish(last)
    y_finish(2)
    for u in range(last):
        sent_y(u)
    d_finish(0)
    d_finish(1)
    sent_d(0)
    sent_d(1)
    sent_c(last)
    y_finish(last)
    d_finish(2)
    sent_d(2)
    sent_y(last)
    d_finish(last)
    sent_d(last)


def body(
    inputs, query_states, key_states, value_states, out_grad, first_flags,
    weight, moment_one, moment_two,
):
    _, tok, width = query_states.shape
    feats = inputs.shape[2]
    heads = width // HEAD_DIM
    rows = weight.shape[0]
    xn = lax.axis_size("clip") // (CORES * YH)
    ys = YN * YH
    half = ZN // CORES
    part = half * rows
    wide = [(hi - lo) * HEAD_DIM for lo, hi in UNITS]
    nu = len(UNITS)
    bf, f32 = jnp.bfloat16, jnp.float32
    V = pltpu.VMEM
    lanes = (tok + 127) // 128 * 128
    dma = pltpu.SemaphoreType.DMA
    scratch = (
        [pltpu.SMEM(first_flags.shape, jnp.int32)]
        + [V((tok + tok // 2, feats), bf), V((feats, tok + tok // 2), bf)]
        + [V((heads, tok, HEAD_DIM), bf)] * 4
        + [V((heads, 2 * tok, HEAD_DIM), bf)] * 2
        + [V((heads, tok, tok), f32)] * 2
        + [V((heads, 8, lanes), f32)] * 4
        + [V((heads, tok + tok // 2, HEAD_DIM), f32)]
        + [V((heads, tok // 2, HEAD_DIM), bf)] * 2
        + [V((CORES, YN, part, w), bf) for w in wide]
        + [V((YN, part, w), bf) for w in wide]
        + [V((YN, part, w), bf) for w in wide]
        + [V((xn - 1, part, w), bf) for w in wide]
        + [V((half, rows, w), f32) for w in wide]
        + [V((ZN - 1, rows, w), f32) for w in wide]
        + [V((rows, w), f32) for w in wide]
        + [V((ys - 1, rows, w), f32) for w in wide]
        + [V((rows, w), f32) for w in wide]
        + [dma((4, heads)), dma((1,)), dma((1,))]
        + [dma((4, heads))] * 2
        + [dma((1,))] * 2
        + [dma((1,))] * 2
        + [dma((heads,))] * 2
        + [pltpu.SemaphoreType.REGULAR((ROUNDS,))]
        + [dma((heads,))] * 2
        + [dma((nu,))] * 2
        + [dma((nu, xn - 1))] * 2
        + [dma((nu, half)), dma((nu, ZN - 1))]
        + [dma((nu, YH)), dma((nu, ys - 1))]
        + [dma((nu, xn, CORES)), dma((nu,))]
    )
    gradient = pl.pallas_call(
        kernel,
        out_shape=jax.ShapeDtypeStruct((rows, width), f32),
        in_specs=[pl.BlockSpec(memory_space=pltpu.HBM)] * 6,
        out_specs=pl.BlockSpec(memory_space=pltpu.VMEM),
        scratch_shapes=scratch,
        compiler_params=pltpu.CompilerParams(
            collective_id=0, has_side_effects=True, vmem_limit_bytes=VMEM_BYTES
        ),
        cost_estimate=pl.CostEstimate(flops=2_000_000_000, bytes_accessed=3_000_000, transcendentals=2_000_000),
    )(inputs, query_states, key_states, value_states, out_grad, first_flags)
    return adamw(weight, moment_one, moment_two, gradient)


def solution(mesh):
    in_specs = (
        P("clip", "tm", None),
        P("clip", "tm", None),
        P("clip", "tm", None),
        P("clip", "tm", None),
        P("clip", "tm", None),
        P("clip", None),
        P("tm", None),
        P("tm", None),
        P("tm", None),
    )
    out_specs = (P("tm", None), P("tm", None), P("tm", None))
    return jax.shard_map(body, mesh=mesh, in_specs=in_specs, out_specs=out_specs, check_vma=False)
```

```python
import functools
import math

import jax
import jax.numpy as jnp
from jax import lax
from jax.experimental import pallas as pl
from jax.experimental.pallas import tpu as pltpu
from jax.sharding import PartitionSpec as P

HEAD_DIM = 128
MESH = pl.DeviceIdType.MESH
NEG = -1e30
VMEM_BYTES = 66_700_000

ZN = 8
YN = 4
YH = 2
CORES = 2
ROUNDS = 3
UNITS = ((0, 2), (2, 4), (4, 5), (5, 6))

beta_one = 0.9
beta_two = 0.95
learn_rate = 0.001
adam_eps = 1e-08
decay_rate = 0.1
step_count = 10.0


def adamw(weight, moment_one, moment_two, gradient):
    new_one = beta_one * moment_one + (1.0 - beta_one) * gradient
    new_two = beta_two * moment_two + (1.0 - beta_two) * gradient * gradient
    corr_one = new_one / (1.0 - beta_one**step_count)
    corr_two = new_two / (1.0 - beta_two**step_count)
    new_weight = weight - learn_rate * (
        corr_one / (jnp.sqrt(corr_two) + adam_eps) + decay_rate * weight
    )
    return (new_weight, new_one, new_two)


def dot_nt(a, b):
    return lax.dot_general(a, b, (((1,), (1,)), ((), ())), preferred_element_type=jnp.float32)


def dot_nn(a, b):
    return lax.dot_general(a, b, (((1,), (0,)), ((), ())), preferred_element_type=jnp.float32)


def kernel(
    x_hbm, q_hbm, k_hbm, v_hbm, g_hbm, flags_hbm,
    grad_out,
    flags, xcat, xt, qo, go, qn, gn, kc, vc,
    e_own, dp_own, own_st, own_st_in, nf_st, nf_st_in, kgn, ret, ret_in,
    *rest,
):
    nu = len(UNITS)
    gbuf, a_in, abuf, b_in, bbuf, c_in, cbuf, y_in, d_in = [rest[i * nu : (i + 1) * nu] for i in range(9)]
    (sem_loc, sem_locx, sem_f, win_s, win_r, x_s, x_r, os_s, os_r, nf_s, nf_r,
     near_sem, ret_s, ret_r, a_s, a_r, b_s, b_r, c_s, c_r, y_s, y_r, d_s, d_r) = rest[9 * nu :]
    heads, tok, _ = qo.shape
    half = ZN // CORES
    rows = grad_out.shape[0]
    part = half * rows
    f32, bf = jnp.float32, jnp.bfloat16
    tm_n = lax.axis_size("tm")
    xn = lax.axis_size("clip") // (CORES * YH)
    ys = YN * YH
    t = lax.axis_index("tm")
    c = lax.axis_index("clip")
    core = lax.rem(c, CORES)
    x = c // (CORES * YH)
    z = lax.rem(t, ZN)
    y = lax.rem(c // CORES, YH) * YN + t // ZN
    y_lo = t // ZN
    holder = z // half == core
    final = jnp.logical_and(holder, x == y_lo)
    has_prev = t > 0
    has_next = t < tm_n - 1
    nxt = jnp.minimum(t + 1, tm_n - 1)
    prv = jnp.maximum(t - 1, 0)
    sibling = c + 1 - 2 * core

    def cols(h):
        return pl.ds(pl.multiple_of(h * HEAD_DIM, HEAD_DIM), HEAD_DIM)

    cut = tok * 2 // 5
    own_rows = pl.ds(0, tok)
    prev_rows = pl.ds(tok, tok)

    def remote(src, dst, ssem, rsem, where):
        return pltpu.make_async_remote_copy(
            src_ref=src, dst_ref=dst, send_sem=ssem, recv_sem=rsem,
            device_id=where, device_id_type=MESH,
        )

    def local_copies(h):
        places = (
            (q_hbm, qo.at[h]), (k_hbm, kc.at[h, own_rows]),
            (v_hbm, vc.at[h, own_rows]), (g_hbm, go.at[h]),
        )
        return [
            pltpu.make_async_copy(src.at[0, :, cols(h)], dst, sem_loc.at[i, h])
            for i, (src, dst) in enumerate(places)
        ]

    def ahead(h):
        return [
            remote(src.at[0, :, cols(h)], dst.at[h, prev_rows], win_s.at[i, h], win_r.at[i, h], {"tm": nxt})
            for i, (src, dst) in enumerate(((k_hbm, kc), (v_hbm, vc)))
        ]

    def behind(h):
        return [
            remote(src.at[0, :, cols(h)], dst.at[h], win_s.at[2 + i, h], win_r.at[2 + i, h], {"tm": prv})
            for i, (src, dst) in enumerate(((q_hbm, qn), (g_hbm, gn)))
        ]

    x_copy = remote(x_hbm.at[0, pl.ds(0, cut)], xcat.at[pl.ds(tok, cut)], x_s.at[0], x_r.at[0], {"tm": nxt})
    x_local = pltpu.make_async_copy(x_hbm.at[0], xcat.at[own_rows], sem_locx.at[0])
    f_local = pltpu.make_async_copy(flags_hbm, flags, sem_f.at[0])
    os_copy = remote(own_st, own_st_in, os_s.at[0], os_r.at[0], {"tm": prv})

    def nf_copy(h):
        return remote(nf_st.at[h], nf_st_in.at[h], nf_s.at[h], nf_r.at[h], {"tm": nxt})

    def ret_copy(h):
        return remote(ret.at[h], ret_in.at[h], ret_s.at[h], ret_r.at[h], {"tm": prv})

    def at_y(to):
        return {"clip": (x * YH + to // YN) * CORES + core, "tm": lax.rem(to, YN) * ZN + z}

    def at_z(to):
        return {"tm": y_lo * ZN + to}

    def at_x(d, to_core):
        return {"clip": lax.rem(x + d, xn) * (YH * CORES) + lax.rem(c, YH * CORES) - core + to_core}

    def a_copy(u):
        return remote(gbuf[u].at[1 - core], a_in[u], a_s.at[u], a_r.at[u], {"clip": sibling})

    def b_copy(u, d):
        return remote(abuf[u].at[lax.rem(x + d, xn)], b_in[u].at[d - 1], b_s.at[u, d - 1], b_r.at[u, d - 1], at_x(d, core))

    def c_copy(u, i):
        to = core * half + i
        slot = lax.rem(to - z + ZN - 1, ZN)
        return remote(bbuf[u].at[i], c_in[u].at[slot], c_s.at[u, i], c_r.at[u, slot], at_z(to))

    def c_arrival(u, slot):
        return remote(bbuf[u].at[0], c_in[u].at[slot], c_s.at[u, 0], c_r.at[u, slot], at_z(lax.rem(z + 1, ZN)))

    def y_copy(u, k):
        to = x + k * YN
        slot = lax.rem(to - y + 2 * ys - 1, ys)
        return remote(cbuf[u], y_in[u].at[slot], y_s.at[u, k], y_r.at[u, slot], at_y(to))

    def y_arrival(u, slot):
        return remote(cbuf[u], y_in[u].at[slot], y_s.at[u, 0], y_r.at[u, slot], at_y(lax.rem(y + 1, ys)))

    def d_copy(u, d, to_core):
        return remote(d_in[u], d_in[u], d_s.at[u, d, to_core], d_r.at[u], at_x(d, to_core))

    def d_near(u):
        return remote(d_in[u], d_in[u], d_s.at[u, 0, 0], d_r.at[u], {"clip": sibling})

    def each(lo, hi, fn):
        def step(i, carry):
            fn(i)
            return carry
        lax.fori_loop(lo, hi, step, 0)

    def start_local(h):
        for cp in local_copies(h):
            cp.start()
    bar = pltpu.get_barrier_semaphore()
    def hello(where):
        pl.semaphore_signal(bar, inc=1, device_id=where, device_id_type=MESH)
    @pl.when(has_prev)
    def _():
        hello({"tm": prv})
    @pl.when(has_next)
    def _():
        hello({"tm": nxt})
    hello({"clip": sibling})
    beside = [
        at_z(lax.rem(z + 1, ZN)), at_z(lax.rem(z + ZN - 1, ZN)),
        at_y(lax.rem(y + 1, ys)), at_y(lax.rem(y + ys - 1, ys)),
        at_x(1, core), at_x(xn - 1, core),
    ]
    for where in beside:
        hello(where)
    count = 1 + len(beside)
    each(0, heads, start_local)
    x_local.start()
    f_local.start()
    pl.semaphore_wait(bar, count + has_prev.astype(jnp.int32) + has_next.astype(jnp.int32))

    def tell(i):
        for where in beside:
            pl.semaphore_signal(near_sem.at[i], inc=1, device_id=where, device_id_type=MESH)

    def hear(i):
        pl.semaphore_wait(near_sem.at[i], len(beside))

    def send_window(h):
        @pl.when(has_next)
        def _():
            for cp in ahead(h):
                cp.start()
        @pl.when(has_prev)
        def _():
            for cp in behind(h):
                cp.start()

    send_window(0)
    @pl.when(has_next)
    def _():
        x_copy.start()
    send_window(1)
    tell(0)

    @pl.when(jnp.logical_not(has_prev))
    def _():
        kc[:, tok : 2 * tok, :] = jnp.zeros((heads, tok, HEAD_DIM), bf)
        vc[:, tok : 2 * tok, :] = jnp.zeros((heads, tok, HEAD_DIM), bf)
        xcat[tok : tok + cut, :] = jnp.zeros((cut, xcat.shape[1]), bf)
        nf_st_in[...] = jnp.zeros_like(nf_st_in)
        nf_st_in[:, 0:1, :] = jnp.full((heads, 1, nf_st_in.shape[2]), NEG, f32)

    @pl.when(jnp.logical_not(has_next))
    def _():
        qn[...] = jnp.zeros_like(qn)
        gn[...] = jnp.zeros_like(gn)
        ret_in[...] = jnp.zeros_like(ret_in)
        own_st_in[...] = jnp.ones_like(own_st_in)

    scaling = 1.0 / math.sqrt(HEAD_DIM)
    to_log2 = scaling * math.log2(math.e)

    def stats(s, dp):
        m = jnp.max(s, axis=0, keepdims=True) * to_log2
        e = jnp.exp2(s * to_log2 - m)
        return e, m, jnp.sum(e, axis=0, keepdims=True), jnp.sum(e * dp, axis=0, keepdims=True)

    def put(ref, h, m, l, d):
        ref[h, 0:1, 0:tok] = m
        ref[h, 1:2, 0:tok] = l
        ref[h, 2:3, 0:tok] = d

    def get(ref, h):
        return ref[h, 0:1, 0:tok], ref[h, 1:2, 0:tok], ref[h, 2:3, 0:tok]

    own_st[...] = jnp.zeros_like(own_st)
    nf_st[...] = jnp.zeros_like(nf_st)

    def own_blocks(i):
        pair = (i * 2, i * 2 + 1)
        for h in pair:
            for cp in local_copies(h):
                cp.wait()
        for h in pair:
            s = dot_nt(kc[h, own_rows], qo[h])
            dp = dot_nt(vc[h, own_rows], go[h])
            e, m, l, d = stats(s, dp)
            e_own[h] = e
            dp_own[h] = dp
            put(own_st, h, m, l, d)
    each(0, heads // 2, own_blocks)

    @pl.when(has_prev)
    def _():
        os_copy.start()
    send_window(2)

    f_local.wait()
    fo = flags[0, t]
    fn = flags[0, nxt]
    near_ok = jnp.logical_and(fn == 0, has_next)
    far_ok = jnp.logical_and(jnp.logical_and(near_ok, fo == 0), has_prev)

    def total(ma, la, da, mb, lb, db):
        mt = jnp.maximum(ma, mb)
        fa = jnp.exp2(ma - mt)
        fb = jnp.exp2(mb - mt)
        inv = 1.0 / (fa * la + fb * lb)
        return fa, fb, inv, (fa * da + fb * db) * inv

    def near_far(h):
        @pl.when(has_prev)
        def _():
            for cp in ahead(h):
                cp.wait_recv()
        @pl.when(has_next)
        def _():
            for cp in behind(h):
                cp.wait_recv()
        qq, gg = qn[h], gn[h]
        s = dot_nt(kc[h], qq)
        dp = dot_nt(vc[h], gg)
        e1, m1, l1, d1 = stats(s[:tok], dp[:tok])
        e2, m2, l2, d2 = stats(s[tok:], dp[tok:])
        zero = jnp.zeros_like(m1)
        m1p = jnp.where(near_ok, m1, NEG)
        m2p = jnp.where(far_ok, m2, NEG)
        mb = jnp.maximum(m1p, m2p)
        f1 = jnp.where(near_ok, jnp.exp2(m1p - mb), zero)
        f2 = jnp.where(far_ok, jnp.exp2(m2p - mb), zero)
        lb = f1 * l1 + f2 * l2
        db = f1 * d1 + f2 * d2
        put(nf_st, h, mb, lb, db)
        @pl.when(has_next)
        def _():
            nf_copy(h).start()
        @pl.when(jnp.logical_and(h == 0, has_next))
        def _():
            os_copy.wait_recv()
        ma, la, da = get(own_st_in, h)
        _, fb, inv, delta = total(ma, la, da, mb, lb, db)
        w = fb * inv * scaling
        ds1 = ((e1 * (f1 * w)) * (dp[:tok] - delta)).astype(bf)
        ds2 = ((e2 * (f2 * w)) * (dp[tok:] - delta)).astype(bf)
        kg = dot_nn(jnp.concatenate([ds1, ds2], axis=0), qq)
        kgn[h] = kg[: tok + cut]
        ret[h] = kg[tok + cut :].astype(bf)
        @pl.when(has_prev)
        def _():
            ret_copy(h).start()
        @pl.when(h + 3 < heads)
        def _():
            send_window(h + 3)

    def finish(h):
        @pl.when(has_prev)
        def _():
            nf_copy(h).wait_recv()
        ma, la, da = get(own_st, h)
        mb, lb, db = get(nf_st_in, h)
        fa, _, inv, delta = total(ma, la, da, mb, lb, db)
        ds = ((e_own[h] * (fa * inv * scaling)) * (dp_own[h] - delta)).astype(bf)
        own = dot_nn(ds, qo[h])
        @pl.when(has_next)
        def _():
            ret_copy(h).wait_recv()
        back = ret_in[h].astype(f32)
        kg = jnp.concatenate(
            [kgn[h, 0:cut] + own[:cut], kgn[h, cut:tok] + own[cut:] + back, kgn[h, tok : tok + cut]], axis=0
        ).astype(bf)
        grad = dot_nn(xt[...], kg).astype(bf)
        for u, (lo, hi) in enumerate(UNITS):
            @pl.when(jnp.logical_and(h >= lo, h < hi))
            def _():
                for yy in range(YN):
                    for k in range(CORES):
                        at = (yy * CORES + k) * part
                        gbuf[u][k, yy, :, cols(h - lo)] = grad[at : at + part]

    def a_finish(u):
        a_copy(u).wait_recv()
        for yy in range(YN):
            abuf[u][yy] = (gbuf[u][core, yy].astype(f32) + a_in[u][yy].astype(f32)).astype(bf)
        each(1, xn, lambda d: b_copy(u, d).start())

    def b_finish(u):
        each(1, xn, lambda d: b_copy(u, d).wait_recv())
        acc = abuf[u][x].astype(f32)
        for d in range(xn - 1):
            acc = acc + b_in[u][d].astype(f32)
        bbuf[u][...] = acc.reshape(bbuf[u].shape)
        def send(i):
            @pl.when(core * half + i != z)
            def _():
                c_copy(u, i).start()
        each(0, half, send)

    def c_finish(u):
        @pl.when(holder)
        def _():
            each(0, ZN - 1, lambda i: c_arrival(u, i).wait_recv())
            acc = bbuf[u][lax.rem(z, half)]
            for i in range(ZN - 1):
                acc = acc + c_in[u][i]
            cbuf[u][...] = acc
            def send(k):
                @pl.when(x + k * YN != y)
                def _():
                    y_copy(u, k).start()
            each(0, YH, send)

    def y_finish(u):
        @pl.when(final)
        def _():
            each(0, ys - 1, lambda i: y_arrival(u, i).wait_recv())
            acc = cbuf[u][...]
            for i in range(ys - 1):
                acc = acc + y_in[u][i]
            d_in[u][...] = acc
            d_near(u).start()
            for k in range(CORES):
                each(1, xn, lambda d: d_copy(u, d, k).start())

    def d_finish(u):
        @pl.when(jnp.logical_not(final))
        def _():
            d_near(u).wait_recv()
        lo, hi = UNITS[u]
        grad_out[:, lo * HEAD_DIM : hi * HEAD_DIM] = d_in[u][...]

    def main(h, carry):
        @pl.when(h < heads)
        def _():
            near_far(h)
        @pl.when(h == 0)
        def _():
            x_local.wait()
            @pl.when(has_prev)
            def _():
                x_copy.wait_recv()
            xt[...] = xcat[...].T
        @pl.when(h == 6)
        def _():
            a_finish(2)
        @pl.when(h > 0)
        def _():
            finish(h - 1)
        @pl.when(h < ROUNDS)
        def _():
            hear(h)
        @pl.when(h < ROUNDS - 1)
        def _():
            tell(h + 1)
        @pl.when(h == 2)
        def _():
            a_copy(0).start()
        @pl.when(h == 3)
        def _():
            a_finish(0)
        @pl.when(h == 4)
        def _():
            a_copy(1).start()
        @pl.when(h == 5)
        def _():
            a_copy(2).start()
            a_finish(1)
        return carry
    lax.fori_loop(0, heads + 1, main, 0)

    def sent_window():
        @pl.when(has_next)
        def _():
            x_copy.wait_send()
            def sent(h):
                for cp in ahead(h):
                    cp.wait_send()
                nf_copy(h).wait_send()
            each(0, heads, sent)
        @pl.when(has_prev)
        def _():
            os_copy.wait_send()
            def sent(h):
                for cp in behind(h):
                    cp.wait_send()
                ret_copy(h).wait_send()
            each(0, heads, sent)

    def sent_ab(u):
        a_copy(u).wait_send()
        each(1, xn, lambda d: b_copy(u, d).wait_send())

    def sent_c(u):
        def left(i):
            @pl.when(core * half + i != z)
            def _():
                c_copy(u, i).wait_send()
        each(0, half, left)

    def sent_y(u):
        @pl.when(holder)
        def _():
            def left(k):
                @pl.when(x + k * YN != y)
                def _():
                    y_copy(u, k).wait_send()
            each(0, YH, left)

    def sent_d(u):
        @pl.when(final)
        def _():
            d_near(u).wait_send()
            for k in range(CORES):
                each(1, xn, lambda d: d_copy(u, d, k).wait_send())

    last = nu - 1
    a_copy(last).start()
    sent_window()
    b_finish(0)
    b_finish(1)
    a_finish(last)
    b_finish(2)
    for u in range(last):
        sent_ab(u)
    c_finish(0)
    c_finish(1)
    b_finish(last)
    c_finish(2)
    sent_ab(last)
    for u in range(last):
        sent_c(u)
    y_finish(0)
    y_finish(1)
    c_finish(last)
    y_finish(2)
    for u in range(last):
        sent_y(u)
    d_finish(0)
    d_finish(1)
    sent_d(0)
    sent_d(1)
    sent_c(last)
    y_finish(last)
    d_finish(2)
    sent_d(2)
    sent_y(last)
    d_finish(last)
    sent_d(last)


def body(
    inputs, query_states, key_states, value_states, out_grad, first_flags,
    weight, moment_one, moment_two,
):
    _, tok, width = query_states.shape
    feats = inputs.shape[2]
    heads = width // HEAD_DIM
    rows = weight.shape[0]
    xn = lax.axis_size("clip") // (CORES * YH)
    ys = YN * YH
    half = ZN // CORES
    part = half * rows
    wide = [(hi - lo) * HEAD_DIM for lo, hi in UNITS]
    nu = len(UNITS)
    bf, f32 = jnp.bfloat16, jnp.float32
    V = pltpu.VMEM
    cut = tok * 2 // 5
    lanes = (tok + 127) // 128 * 128
    dma = pltpu.SemaphoreType.DMA
    scratch = (
        [pltpu.SMEM(first_flags.shape, jnp.int32)]
        + [V((tok + cut, feats), bf), V((feats, tok + cut), bf)]
        + [V((heads, tok, HEAD_DIM), bf)] * 4
        + [V((heads, 2 * tok, HEAD_DIM), bf)] * 2
        + [V((heads, tok, tok), f32)] * 2
        + [V((heads, 8, lanes), f32)] * 4
        + [V((heads, tok + cut, HEAD_DIM), f32)]
        + [V((heads, tok - cut, HEAD_DIM), bf)] * 2
        + [V((CORES, YN, part, w), bf) for w in wide]
        + [V((YN, part, w), bf) for w in wide]
        + [V((YN, part, w), bf) for w in wide]
        + [V((xn - 1, part, w), bf) for w in wide]
        + [V((half, rows, w), f32) for w in wide]
        + [V((ZN - 1, rows, w), f32) for w in wide]
        + [V((rows, w), f32) for w in wide]
        + [V((ys - 1, rows, w), f32) for w in wide]
        + [V((rows, w), f32) for w in wide]
        + [dma((4, heads)), dma((1,)), dma((1,))]
        + [dma((4, heads))] * 2
        + [dma((1,))] * 2
        + [dma((1,))] * 2
        + [dma((heads,))] * 2
        + [pltpu.SemaphoreType.REGULAR((ROUNDS,))]
        + [dma((heads,))] * 2
        + [dma((nu,))] * 2
        + [dma((nu, xn - 1))] * 2
        + [dma((nu, half)), dma((nu, ZN - 1))]
        + [dma((nu, YH)), dma((nu, ys - 1))]
        + [dma((nu, xn, CORES)), dma((nu,))]
    )
    gradient = pl.pallas_call(
        kernel,
        out_shape=jax.ShapeDtypeStruct((rows, width), f32),
        in_specs=[pl.BlockSpec(memory_space=pltpu.HBM)] * 6,
        out_specs=pl.BlockSpec(memory_space=pltpu.VMEM),
        scratch_shapes=scratch,
        compiler_params=pltpu.CompilerParams(
            collective_id=0, has_side_effects=True, vmem_limit_bytes=VMEM_BYTES
        ),
        cost_estimate=pl.CostEstimate(flops=2_000_000_000, bytes_accessed=3_000_000, transcendentals=2_000_000),
    )(inputs, query_states, key_states, value_states, out_grad, first_flags)
    return adamw(weight, moment_one, moment_two, gradient)


def solution(mesh):
    in_specs = (
        P("clip", "tm", None),
        P("clip", "tm", None),
        P("clip", "tm", None),
        P("clip", "tm", None),
        P("clip", "tm", None),
        P("clip", None),
        P("tm", None),
        P("tm", None),
        P("tm", None),
    )
    out_specs = (P("tm", None), P("tm", None), P("tm", None))
    return jax.shard_map(body, mesh=mesh, in_specs=in_specs, out_specs=out_specs, check_vma=False)
```

```python
import functools
import math

import jax
import jax.numpy as jnp
from jax import lax
from jax.experimental import pallas as pl
from jax.experimental.pallas import tpu as pltpu
from jax.sharding import PartitionSpec as P

HEAD_DIM = 128
MESH = pl.DeviceIdType.MESH
NEG = -1e30
VMEM_BYTES = 66_700_000

ZN = 8
YN = 4
YH = 2
CORES = 2
ROUNDS = 3
UNITS = ((0, 2), (2, 4), (4, 5), (5, 6))

beta_one = 0.9
beta_two = 0.95
learn_rate = 0.001
adam_eps = 1e-08
decay_rate = 0.1
step_count = 10.0


def adamw(weight, moment_one, moment_two, gradient):
    new_one = beta_one * moment_one + (1.0 - beta_one) * gradient
    new_two = beta_two * moment_two + (1.0 - beta_two) * gradient * gradient
    corr_one = new_one / (1.0 - beta_one**step_count)
    corr_two = new_two / (1.0 - beta_two**step_count)
    new_weight = weight - learn_rate * (
        corr_one / (jnp.sqrt(corr_two) + adam_eps) + decay_rate * weight
    )
    return (new_weight, new_one, new_two)


def dot_nt(a, b):
    return lax.dot_general(a, b, (((1,), (1,)), ((), ())), preferred_element_type=jnp.float32)


def dot_nn(a, b):
    return lax.dot_general(a, b, (((1,), (0,)), ((), ())), preferred_element_type=jnp.float32)


def kernel(
    x_hbm, q_hbm, k_hbm, v_hbm, g_hbm, flags_hbm,
    grad_out,
    flags, xcat, xt, qo, go, qn, gn, kc, vc,
    e_own, dp_own, own_st, own_st_in, nf_st, nf_st_in, kgn, ret, ret_in,
    *rest,
):
    nu = len(UNITS)
    gbuf, a_in, abuf, b_in, bbuf, c_in, cbuf, y_in, d_in = [rest[i * nu : (i + 1) * nu] for i in range(9)]
    (sem_loc, sem_locx, sem_f, win_s, win_r, x_s, x_r, os_s, os_r, nf_s, nf_r,
     near_sem, ret_s, ret_r, a_s, a_r, b_s, b_r, c_s, c_r, y_s, y_r, d_s, d_r) = rest[9 * nu :]
    heads, tok, _ = qo.shape
    half = ZN // CORES
    rows = grad_out.shape[0]
    part = half * rows
    f32, bf = jnp.float32, jnp.bfloat16
    tm_n = lax.axis_size("tm")
    xn = lax.axis_size("clip") // (CORES * YH)
    ys = YN * YH
    t = lax.axis_index("tm")
    c = lax.axis_index("clip")
    core = lax.rem(c, CORES)
    x = c // (CORES * YH)
    z = lax.rem(t, ZN)
    y = lax.rem(c // CORES, YH) * YN + t // ZN
    y_lo = t // ZN
    holder = z // half == core
    final = jnp.logical_and(holder, x == y_lo)
    has_prev = t > 0
    has_next = t < tm_n - 1
    nxt = jnp.minimum(t + 1, tm_n - 1)
    prv = jnp.maximum(t - 1, 0)
    sibling = c + 1 - 2 * core

    def cols(h):
        return pl.ds(pl.multiple_of(h * HEAD_DIM, HEAD_DIM), HEAD_DIM)

    cut = tok * 2 // 5
    own_rows = pl.ds(0, tok)
    prev_rows = pl.ds(tok, tok)

    def remote(src, dst, ssem, rsem, where):
        return pltpu.make_async_remote_copy(
            src_ref=src, dst_ref=dst, send_sem=ssem, recv_sem=rsem,
            device_id=where, device_id_type=MESH,
        )

    def local_copies(h):
        places = (
            (q_hbm, qo.at[h]), (k_hbm, kc.at[h, own_rows]),
            (v_hbm, vc.at[h, own_rows]), (g_hbm, go.at[h]),
        )
        return [
            pltpu.make_async_copy(src.at[0, :, cols(h)], dst, sem_loc.at[i, h])
            for i, (src, dst) in enumerate(places)
        ]

    def ahead(h):
        return [
            remote(src.at[0, :, cols(h)], dst.at[h, prev_rows], win_s.at[i, h], win_r.at[i, h], {"tm": nxt})
            for i, (src, dst) in enumerate(((k_hbm, kc), (v_hbm, vc)))
        ]

    def behind(h):
        return [
            remote(src.at[0, :, cols(h)], dst.at[h], win_s.at[2 + i, h], win_r.at[2 + i, h], {"tm": prv})
            for i, (src, dst) in enumerate(((q_hbm, qn), (g_hbm, gn)))
        ]

    x_copy = remote(x_hbm.at[0, pl.ds(0, cut)], xcat.at[pl.ds(tok, cut)], x_s.at[0], x_r.at[0], {"tm": nxt})
    x_local = pltpu.make_async_copy(x_hbm.at[0], xcat.at[own_rows], sem_locx.at[0])
    f_local = pltpu.make_async_copy(flags_hbm, flags, sem_f.at[0])
    os_copy = remote(own_st, own_st_in, os_s.at[0], os_r.at[0], {"tm": prv})

    def nf_copy(h):
        return remote(nf_st.at[h], nf_st_in.at[h], nf_s.at[h], nf_r.at[h], {"tm": nxt})

    def ret_copy(h):
        return remote(ret.at[h], ret_in.at[h], ret_s.at[h], ret_r.at[h], {"tm": prv})

    def at_y(to):
        return {"clip": (x * YH + to // YN) * CORES + core, "tm": lax.rem(to, YN) * ZN + z}

    def at_z(to):
        return {"tm": y_lo * ZN + to}

    def at_x(d, to_core):
        return {"clip": lax.rem(x + d, xn) * (YH * CORES) + lax.rem(c, YH * CORES) - core + to_core}

    def a_copy(u):
        return remote(gbuf[u].at[1 - core], a_in[u], a_s.at[u], a_r.at[u], {"clip": sibling})

    def b_copy(u, d):
        return remote(abuf[u].at[lax.rem(x + d, xn)], b_in[u].at[d - 1], b_s.at[u, d - 1], b_r.at[u, d - 1], at_x(d, core))

    def c_copy(u, i):
        to = core * half + i
        slot = lax.rem(to - z + ZN - 1, ZN)
        return remote(bbuf[u].at[i], c_in[u].at[slot], c_s.at[u, i], c_r.at[u, slot], at_z(to))

    def c_arrival(u, slot):
        return remote(bbuf[u].at[0], c_in[u].at[slot], c_s.at[u, 0], c_r.at[u, slot], at_z(lax.rem(z + 1, ZN)))

    def y_copy(u, k):
        to = x + k * YN
        slot = lax.rem(to - y + 2 * ys - 1, ys)
        return remote(cbuf[u], y_in[u].at[slot], y_s.at[u, k], y_r.at[u, slot], at_y(to))

    def y_arrival(u, slot):
        return remote(cbuf[u], y_in[u].at[slot], y_s.at[u, 0], y_r.at[u, slot], at_y(lax.rem(y + 1, ys)))

    def d_copy(u, d, to_core):
        return remote(d_in[u], d_in[u], d_s.at[u, d, to_core], d_r.at[u], at_x(d, to_core))

    def d_near(u):
        return remote(d_in[u], d_in[u], d_s.at[u, 0, 0], d_r.at[u], {"clip": sibling})

    def each(lo, hi, fn):
        def step(i, carry):
            fn(i)
            return carry
        lax.fori_loop(lo, hi, step, 0)

    def start_local(h):
        for cp in local_copies(h):
            cp.start()
    bar = pltpu.get_barrier_semaphore()
    def hello(where):
        pl.semaphore_signal(bar, inc=1, device_id=where, device_id_type=MESH)
    @pl.when(has_prev)
    def _():
        hello({"tm": prv})
    @pl.when(has_next)
    def _():
        hello({"tm": nxt})
    hello({"clip": sibling})
    beside = [
        at_z(lax.rem(z + 1, ZN)), at_z(lax.rem(z + ZN - 1, ZN)),
        at_y(lax.rem(y + 1, ys)), at_y(lax.rem(y + ys - 1, ys)),
        at_x(1, core), at_x(xn - 1, core),
    ]
    for where in beside:
        hello(where)
    count = 1 + len(beside)
    each(0, heads, start_local)
    x_local.start()
    f_local.start()
    pl.semaphore_wait(bar, count + has_prev.astype(jnp.int32) + has_next.astype(jnp.int32))

    def tell(i):
        for where in beside:
            pl.semaphore_signal(near_sem.at[i], inc=1, device_id=where, device_id_type=MESH)

    def hear(i):
        pl.semaphore_wait(near_sem.at[i], len(beside))

    def send_window(h):
        @pl.when(has_next)
        def _():
            for cp in ahead(h):
                cp.start()
        @pl.when(has_prev)
        def _():
            for cp in behind(h):
                cp.start()

    send_window(0)
    @pl.when(has_next)
    def _():
        x_copy.start()
    send_window(1)
    tell(0)

    @pl.when(jnp.logical_not(has_prev))
    def _():
        kc[:, tok : 2 * tok, :] = jnp.zeros((heads, tok, HEAD_DIM), bf)
        vc[:, tok : 2 * tok, :] = jnp.zeros((heads, tok, HEAD_DIM), bf)
        xcat[tok : tok + cut, :] = jnp.zeros((cut, xcat.shape[1]), bf)
        nf_st_in[...] = jnp.zeros_like(nf_st_in)
        nf_st_in[:, 0:1, :] = jnp.full((heads, 1, nf_st_in.shape[2]), NEG, f32)

    @pl.when(jnp.logical_not(has_next))
    def _():
        qn[...] = jnp.zeros_like(qn)
        gn[...] = jnp.zeros_like(gn)
        ret_in[...] = jnp.zeros_like(ret_in)
        own_st_in[...] = jnp.ones_like(own_st_in)

    scaling = 1.0 / math.sqrt(HEAD_DIM)
    to_log2 = scaling * math.log2(math.e)

    def stats(s, dp):
        m = jnp.max(s, axis=0, keepdims=True) * to_log2
        e = jnp.exp2(s * to_log2 - m)
        return e, m, jnp.sum(e, axis=0, keepdims=True), jnp.sum(e * dp, axis=0, keepdims=True)

    def put(ref, h, m, l, d):
        ref[h, 0:1, 0:tok] = m
        ref[h, 1:2, 0:tok] = l
        ref[h, 2:3, 0:tok] = d

    def get(ref, h):
        return ref[h, 0:1, 0:tok], ref[h, 1:2, 0:tok], ref[h, 2:3, 0:tok]

    own_st[...] = jnp.zeros_like(own_st)
    nf_st[...] = jnp.zeros_like(nf_st)

    def own_blocks(i):
        pair = (i * 2, i * 2 + 1)
        for h in pair:
            for cp in local_copies(h):
                cp.wait()
        for h in pair:
            s = dot_nt(kc[h, own_rows], qo[h])
            dp = dot_nt(vc[h, own_rows], go[h])
            e, m, l, d = stats(s, dp)
            e_own[h] = e
            dp_own[h] = dp
            put(own_st, h, m, l, d)
    each(0, heads // 2, own_blocks)

    @pl.when(has_prev)
    def _():
        os_copy.start()
    send_window(2)

    f_local.wait()
    fo = flags[0, t]
    fn = flags[0, nxt]
    near_ok = jnp.logical_and(fn == 0, has_next)
    far_ok = jnp.logical_and(jnp.logical_and(near_ok, fo == 0), has_prev)

    def total(ma, la, da, mb, lb, db):
        mt = jnp.maximum(ma, mb)
        fa = jnp.exp2(ma - mt)
        fb = jnp.exp2(mb - mt)
        inv = 1.0 / (fa * la + fb * lb)
        return fa, fb, inv, (fa * da + fb * db) * inv

    def near_far(h):
        @pl.when(has_prev)
        def _():
            for cp in ahead(h):
                cp.wait_recv()
        @pl.when(has_next)
        def _():
            for cp in behind(h):
                cp.wait_recv()
        qq, gg = qn[h], gn[h]
        s = dot_nt(kc[h], qq)
        dp = dot_nt(vc[h], gg)
        e1, m1, l1, d1 = stats(s[:tok], dp[:tok])
        e2, m2, l2, d2 = stats(s[tok:], dp[tok:])
        zero = jnp.zeros_like(m1)
        m1p = jnp.where(near_ok, m1, NEG)
        m2p = jnp.where(far_ok, m2, NEG)
        mb = jnp.maximum(m1p, m2p)
        f1 = jnp.where(near_ok, jnp.exp2(m1p - mb), zero)
        f2 = jnp.where(far_ok, jnp.exp2(m2p - mb), zero)
        lb = f1 * l1 + f2 * l2
        db = f1 * d1 + f2 * d2
        put(nf_st, h, mb, lb, db)
        @pl.when(has_next)
        def _():
            nf_copy(h).start()
        @pl.when(jnp.logical_and(h == 0, has_next))
        def _():
            os_copy.wait_recv()
        ma, la, da = get(own_st_in, h)
        _, fb, inv, delta = total(ma, la, da, mb, lb, db)
        w = fb * inv * scaling
        ds1 = ((e1 * (f1 * w)) * (dp[:tok] - delta)).astype(bf)
        ds2 = ((e2 * (f2 * w)) * (dp[tok:] - delta)).astype(bf)
        kg = dot_nn(jnp.concatenate([ds1, ds2], axis=0), qq)
        kgn[h] = kg[: tok + cut]
        ret[h] = kg[tok + cut :].astype(bf)
        @pl.when(has_prev)
        def _():
            ret_copy(h).start()
        @pl.when(h + 3 < heads)
        def _():
            send_window(h + 3)

    def finish(h):
        @pl.when(has_prev)
        def _():
            nf_copy(h).wait_recv()
        ma, la, da = get(own_st, h)
        mb, lb, db = get(nf_st_in, h)
        fa, _, inv, delta = total(ma, la, da, mb, lb, db)
        ds = ((e_own[h] * (fa * inv * scaling)) * (dp_own[h] - delta)).astype(bf)
        own = dot_nn(ds, qo[h])
        @pl.when(has_next)
        def _():
            ret_copy(h).wait_recv()
        back = ret_in[h].astype(f32)
        kg = jnp.concatenate(
            [kgn[h, 0:cut] + own[:cut], kgn[h, cut:tok] + own[cut:] + back, kgn[h, tok : tok + cut]], axis=0
        ).astype(bf)
        grad = dot_nn(xt[...], kg).astype(bf)
        for u, (lo, hi) in enumerate(UNITS):
            @pl.when(jnp.logical_and(h >= lo, h < hi))
            def _():
                for yy in range(YN):
                    for k in range(CORES):
                        at = (yy * CORES + k) * part
                        gbuf[u][k, yy, :, cols(h - lo)] = grad[at : at + part]

    def a_finish(u):
        a_copy(u).wait_recv()
        for yy in range(YN):
            abuf[u][yy] = (gbuf[u][core, yy].astype(f32) + a_in[u][yy].astype(f32)).astype(bf)
        each(1, xn, lambda d: b_copy(u, d).start())

    def b_finish(u):
        each(1, xn, lambda d: b_copy(u, d).wait_recv())
        acc = abuf[u][x].astype(f32)
        for d in range(xn - 1):
            acc = acc + b_in[u][d].astype(f32)
        bbuf[u][...] = acc.reshape(bbuf[u].shape)
        def send(i):
            @pl.when(core * half + i != z)
            def _():
                c_copy(u, i).start()
        each(0, half, send)

    def c_finish(u):
        @pl.when(holder)
        def _():
            each(0, ZN - 1, lambda i: c_arrival(u, i).wait_recv())
            acc = bbuf[u][lax.rem(z, half)]
            for i in range(ZN - 1):
                acc = acc + c_in[u][i]
            cbuf[u][...] = acc
            def send(k):
                @pl.when(x + k * YN != y)
                def _():
                    y_copy(u, k).start()
            each(0, YH, send)

    def y_finish(u):
        @pl.when(final)
        def _():
            each(0, ys - 1, lambda i: y_arrival(u, i).wait_recv())
            acc = cbuf[u][...]
            for i in range(ys - 1):
                acc = acc + y_in[u][i]
            d_in[u][...] = acc
            d_near(u).start()
            for k in range(CORES):
                each(1, xn, lambda d: d_copy(u, d, k).start())

    def d_finish(u):
        @pl.when(jnp.logical_not(final))
        def _():
            d_near(u).wait_recv()
        lo, hi = UNITS[u]
        grad_out[:, lo * HEAD_DIM : hi * HEAD_DIM] = d_in[u][...]

    def main(h, carry):
        @pl.when(h < heads)
        def _():
            near_far(h)
        @pl.when(h == 0)
        def _():
            x_local.wait()
            @pl.when(has_prev)
            def _():
                x_copy.wait_recv()
            xt[...] = xcat[...].T
        @pl.when(h == 6)
        def _():
            a_finish(2)
        @pl.when(h > 0)
        def _():
            finish(h - 1)
        @pl.when(h < ROUNDS)
        def _():
            hear(h)
        @pl.when(h < ROUNDS - 1)
        def _():
            tell(h + 1)
        @pl.when(h == 2)
        def _():
            a_copy(0).start()
        @pl.when(h == 3)
        def _():
            a_finish(0)
        @pl.when(h == 4)
        def _():
            a_copy(1).start()
        @pl.when(h == 5)
        def _():
            a_copy(2).start()
            a_finish(1)
        return carry
    lax.fori_loop(0, heads + 1, main, 0)

    def sent_window():
        @pl.when(has_next)
        def _():
            x_copy.wait_send()
            def sent(h):
                for cp in ahead(h):
                    cp.wait_send()
                nf_copy(h).wait_send()
            each(0, heads, sent)
        @pl.when(has_prev)
        def _():
            os_copy.wait_send()
            def sent(h):
                for cp in behind(h):
                    cp.wait_send()
                ret_copy(h).wait_send()
            each(0, heads, sent)

    def sent_ab(u):
        a_copy(u).wait_send()
        each(1, xn, lambda d: b_copy(u, d).wait_send())

    def sent_c(u):
        def left(i):
            @pl.when(core * half + i != z)
            def _():
                c_copy(u, i).wait_send()
        each(0, half, left)

    def sent_y(u):
        @pl.when(holder)
        def _():
            def left(k):
                @pl.when(x + k * YN != y)
                def _():
                    y_copy(u, k).wait_send()
            each(0, YH, left)

    def sent_d(u):
        @pl.when(final)
        def _():
            d_near(u).wait_send()
            for k in range(CORES):
                each(1, xn, lambda d: d_copy(u, d, k).wait_send())

    last = nu - 1
    a_copy(last).start()
    sent_window()
    b_finish(0)
    b_finish(1)
    a_finish(last)
    b_finish(2)
    for u in range(last):
        sent_ab(u)
    b_finish(last)
    c_finish(0)
    c_finish(1)
    c_finish(2)
    sent_ab(last)
    for u in range(last):
        sent_c(u)
    c_finish(last)
    y_finish(0)
    y_finish(1)
    y_finish(2)
    sent_c(last)
    for u in range(last):
        sent_y(u)
    y_finish(last)
    sent_y(last)
    for u in range(nu):
        d_finish(u)
    for u in range(nu):
        sent_d(u)


def body(
    inputs, query_states, key_states, value_states, out_grad, first_flags,
    weight, moment_one, moment_two,
):
    _, tok, width = query_states.shape
    feats = inputs.shape[2]
    heads = width // HEAD_DIM
    rows = weight.shape[0]
    xn = lax.axis_size("clip") // (CORES * YH)
    ys = YN * YH
    half = ZN // CORES
    part = half * rows
    wide = [(hi - lo) * HEAD_DIM for lo, hi in UNITS]
    nu = len(UNITS)
    bf, f32 = jnp.bfloat16, jnp.float32
    V = pltpu.VMEM
    cut = tok * 2 // 5
    lanes = (tok + 127) // 128 * 128
    dma = pltpu.SemaphoreType.DMA
    scratch = (
        [pltpu.SMEM(first_flags.shape, jnp.int32)]
        + [V((tok + cut, feats), bf), V((feats, tok + cut), bf)]
        + [V((heads, tok, HEAD_DIM), bf)] * 4
        + [V((heads, 2 * tok, HEAD_DIM), bf)] * 2
        + [V((heads, tok, tok), f32)] * 2
        + [V((heads, 8, lanes), f32)] * 4
        + [V((heads, tok + cut, HEAD_DIM), f32)]
        + [V((heads, tok - cut, HEAD_DIM), bf)] * 2
        + [V((CORES, YN, part, w), bf) for w in wide]
        + [V((YN, part, w), bf) for w in wide]
        + [V((YN, part, w), bf) for w in wide]
        + [V((xn - 1, part, w), bf) for w in wide]
        + [V((half, rows, w), f32) for w in wide]
        + [V((ZN - 1, rows, w), f32) for w in wide]
        + [V((rows, w), f32) for w in wide]
        + [V((ys - 1, rows, w), f32) for w in wide]
        + [V((rows, w), f32) for w in wide]
        + [dma((4, heads)), dma((1,)), dma((1,))]
        + [dma((4, heads))] * 2
        + [dma((1,))] * 2
        + [dma((1,))] * 2
        + [dma((heads,))] * 2
        + [pltpu.SemaphoreType.REGULAR((ROUNDS,))]
        + [dma((heads,))] * 2
        + [dma((nu,))] * 2
        + [dma((nu, xn - 1))] * 2
        + [dma((nu, half)), dma((nu, ZN - 1))]
        + [dma((nu, YH)), dma((nu, ys - 1))]
        + [dma((nu, xn, CORES)), dma((nu,))]
    )
    gradient = pl.pallas_call(
        kernel,
        out_shape=jax.ShapeDtypeStruct((rows, width), f32),
        in_specs=[pl.BlockSpec(memory_space=pltpu.HBM)] * 6,
        out_specs=pl.BlockSpec(memory_space=pltpu.VMEM),
        scratch_shapes=scratch,
        compiler_params=pltpu.CompilerParams(
            collective_id=0, has_side_effects=True, vmem_limit_bytes=VMEM_BYTES
        ),
        cost_estimate=pl.CostEstimate(flops=2_000_000_000, bytes_accessed=3_000_000, transcendentals=2_000_000),
    )(inputs, query_states, key_states, value_states, out_grad, first_flags)
    return adamw(weight, moment_one, moment_two, gradient)


def solution(mesh):
    in_specs = (
        P("clip", "tm", None),
        P("clip", "tm", None),
        P("clip", "tm", None),
        P("clip", "tm", None),
        P("clip", "tm", None),
        P("clip", None),
        P("tm", None),
        P("tm", None),
        P("tm", None),
    )
    out_specs = (P("tm", None), P("tm", None), P("tm", None))
    return jax.shard_map(body, mesh=mesh, in_specs=in_specs, out_specs=out_specs, check_vma=False)
```
